512 devices in a mesh: band: 16 (over y, core), tan: 32 (over x, z).
Axes of the slice: x: 4, y: 8, z: 8, core: 2. Of those that a mesh axis runs over, the one named last changes fastest.
Arguments:
- grid: bfloat16 [128, 2, 1280, 2560], P('tan', None, 'band'), may hold values from -6 to 6
- trunc: int32 [1280], P('band'), may hold values from 0 to 1279
- wlist: int32 [16], replicated, may hold values from 0 to 639, as said below
- leg_even: bfloat16 [16, 640, 641], P('band'), may hold values from -0.25 to 0.25
- leg_odd: bfloat16 [16, 640, 640], P('band'), may hold values from -0.25 to 0.25
Outputs:
- even_coeffs: float32 [16, 128, 2, 2, 641], P('band', 'tan')
- odd_coeffs: float32 [16, 128, 2, 2, 640], P('band', 'tan')
- inner: float32 [128, 128], P(None, 'tan')
The draws below stay inside these ranges and needn't reach their ends.
Inputs may be any that keep to these rules, and one draw needn't show every extreme that they name: Distinct values; band index b owns wavenumbers wlist[b] and 1279 - wlist[b]; wavenumbers 0 and 639 are always owned.
All inputs are finite; a program needn't handle non-finite values.
Results may differ from the reference program's by a relative error of at most 0.0051.
Values may be sent and summed in bfloat16 or wider, within the bound.
No kernel may reach another device: no remote copies, remote signals or barrier semaphores. Data moves between devices by JAX's collectives and lax.ppermute only.
A program may use at most 64 MiB of HBM per device.

```python
import math
import jax
import jax.numpy as jnp
from jax import lax

NLAT = 1280
NLON = 2560
HALF = 640
DEG_E = 641
DEG_O = 640
PAIRS = 16
NVEC = 128


def draw_wlist(key, part):
    key = jax.random.fold_in(key, 7)
    middle = jax.random.permutation(key, HALF - 2)[:PAIRS].astype(jnp.int32) + 1
    places = jax.random.permutation(jax.random.fold_in(key, 1), PAIRS)[:2]
    middle = middle.at[places[0]].set(0)
    middle = middle.at[places[1]].set(HALF - 1)
    return middle.astype(jnp.int32)


def draw_trunc(key, part):
    key = jax.random.fold_in(key, 11)
    latitude = jnp.arange(NLAT, dtype=jnp.int32)
    polar = 2 * jnp.minimum(latitude, NLAT - 1 - latitude)
    extra = jax.random.randint(key, (NLAT,), 0, NLAT // 16 + 1, dtype=jnp.int32)
    return jnp.minimum(NLAT - 1, polar + extra).astype(jnp.int32)


def levels(key, extent, split, smallest, top_value):
    def one(dim, blocks):
        draws = jax.random.uniform(jax.random.fold_in(jax.random.fold_in(key, 6), dim), (blocks,), jnp.float32, smallest / len(split), top_value / len(split))
        return jnp.repeat(jnp.exp(draws), extent[dim] // blocks).reshape((-1,) + (1,) * (len(extent) - dim - 1))

    loudness = one(*split[0])
    for cut in split[1:]:
        loudness = loudness * one(*cut)
    return loudness


def bell_draw(key, shape, scale, limit, shards=(), kind=jnp.bfloat16):
    values = jax.random.normal(key, shape, jnp.float32) * scale
    if len(shards) > 0:
        values = levels(key, shape, shards, -0.22, 0.18) * values
    return jnp.clip(values, min=-limit, max=limit).astype(kind)


def setup_inputs(seed: int = 0) -> dict:
    key_list = jax.random.split(jax.random.key(seed), 6)
    return {
        "grid": bell_draw(key_list[0], (NVEC, 2, NLAT, NLON), 1.0, 6.0, ((0, 32), (2, 16))),
        "trunc": draw_trunc(jax.random.fold_in(key_list[5], 71), 0),
        "wlist": draw_wlist(jax.random.fold_in(key_list[5], 71), 0),
        "leg_even": bell_draw(key_list[3], (PAIRS, HALF, DEG_E), HALF ** -0.5, 0.25, ((0, 16),)),
        "leg_odd": bell_draw(key_list[4], (PAIRS, HALF, DEG_O), HALF ** -0.5, 0.25, ((0, 16),)),
    }


def fourier_table(mvals):
    longitude = jnp.arange(NLON, dtype=jnp.int32)
    phase = mvals[:, :, None] * longitude[None, None, :] % NLON
    angle = phase.astype(jnp.float32) * (2.0 * math.pi / NLON)
    scaling = 1.0 / math.sqrt(NLON)
    table = jnp.stack([jnp.cos(angle) * scaling, -jnp.sin(angle) * scaling], axis=2)
    return table.astype(jnp.bfloat16)

def reference(grid, trunc, wlist, leg_even, leg_odd):
    mvals = jnp.stack([wlist, NLAT - 1 - wlist], axis=1).astype(jnp.int32)
    table = fourier_table(mvals).astype(jnp.float32)
    keeper = (mvals[None, :, :] <= trunc[:, None, None]).astype(jnp.float32)

    def one_vector(fields):
        spectra = jnp.einsum('fjk,bprk->fjbpr', fields.astype(jnp.float32), table)
        lat_rows = (spectra * keeper[None, :, :, :, None]).astype(jnp.bfloat16)
        northern = lat_rows[:, :HALF].astype(jnp.float32)
        southern = lat_rows[:, HALF:][:, ::-1].astype(jnp.float32)
        return ((northern + southern).astype(jnp.bfloat16), (northern - southern).astype(jnp.bfloat16))
    sym_rows, anti_rows = lax.map(one_vector, grid)
    even_all = jnp.einsum('vfjbpr,bjc->bpvfrc', sym_rows.astype(jnp.float32), leg_even.astype(jnp.float32))
    odd_all = jnp.einsum('vfjbpr,bjc->bpvfrc', anti_rows.astype(jnp.float32), leg_odd.astype(jnp.float32))
    even_bound = (NLAT + 1 - wlist) // 2
    odd_bound = (NLAT - wlist) // 2
    even_cols = jnp.arange(DEG_E, dtype=jnp.int32)
    odd_cols = jnp.arange(DEG_O, dtype=jnp.int32)
    even_pick = (even_cols[None, :] < even_bound[:, None])[:, None, None, None, :]
    odd_pick = (odd_cols[None, :] < odd_bound[:, None])[:, None, None, None, :]
    even_coeffs = jnp.where(even_pick, even_all[:, 0], even_all[:, 1])
    odd_coeffs = jnp.where(odd_pick, odd_all[:, 0], odd_all[:, 1])
    packed = jnp.concatenate([even_coeffs, odd_coeffs], axis=-1).astype(jnp.bfloat16)
    flat_rows = jnp.transpose(packed, (1, 0, 2, 3, 4)).reshape(NVEC, -1)
    inner = jnp.dot(flat_rows, flat_rows.T, preferred_element_type=jnp.float32) / (PAIRS * 4.0 * (NLAT + 1))
    return (even_coeffs, odd_coeffs, inner)
```

```python
import math

import jax
import jax.numpy as jnp
from jax import lax
from jax.experimental import pallas as pl
from jax.experimental.pallas import tpu as pltpu
from jax.sharding import PartitionSpec as P

F32 = jnp.float32
BF16 = jnp.bfloat16
NT = (((1,), (1,)), ((), ()))
NN = (((1,), (0,)), ((), ()))


def fourier_kernel(wlist_ref, trunc_ref, grid_ref, out_ref, table, rows):
    vectors, fields, lats, lons = grid_ref.shape
    bands = wlist_ref.shape[0]
    total_lat = lats * bands
    members = 2 * bands
    row = lax.broadcasted_iota(jnp.int32, (members, 128), 0)
    lane = lax.broadcasted_iota(jnp.int32, (members, 128), 1)
    mvals = jnp.zeros((members, 128), jnp.int32)
    for b in range(bands):
        wave = wlist_ref[b]
        mvals = jnp.where(row == b, wave, mvals)
        mvals = jnp.where(row == bands + b, total_lat - 1 - wave, mvals)
    unit = 2.0 * math.pi / lons
    scaling = 1.0 / math.sqrt(lons)
    chunks = lons // 128
    fine = (mvals * lane % lons).astype(F32) * unit
    coarse = (mvals * lane % chunks).astype(F32) * (128.0 * unit)
    fine_cos, fine_sin = jnp.cos(fine), jnp.sin(fine)
    coarse_cos, coarse_sin = jnp.cos(coarse) * scaling, jnp.sin(coarse) * scaling
    for i in range(chunks):
        cc, cs = coarse_cos[:, i : i + 1], coarse_sin[:, i : i + 1]
        table[:members, 128 * i : 128 * (i + 1)] = (cc * fine_cos - cs * fine_sin).astype(BF16)
        table[members:, 128 * i : 128 * (i + 1)] = (-(cs * fine_cos + cc * fine_sin)).astype(BF16)
    keep = mvals[:, :lats] <= trunc_ref[...]
    keep = jnp.concatenate([keep, keep], axis=0)
    depth = 4 * vectors * fields
    for v in range(vectors):
        for f in range(fields):
            spectra = lax.dot_general(table[...], grid_ref[v, f], NT, preferred_element_type=F32)
            spectra = jnp.where(keep, spectra, 0.0)
            spectra = jnp.pad(spectra, ((0, 0), (0, 128 - lats)))
            for r in range(2):
                for p in range(2):
                    place = ((p * fields + f) * 2 + r) * vectors + v
                    start = (r * 2 + p) * bands
                    rows[pl.ds(place, bands, stride=depth), :] = spectra[start : start + bands]
    out_ref[...] = rows[...].astype(BF16).reshape(out_ref.shape)


def legendre_kernel(wlist_ref, rows_ref, even_t_ref, odd_ref, even_ref, odd_out_ref, send_ref, fold):
    bands, depth, _ = rows_ref.shape
    half_bands = bands // 2
    hemisphere = odd_ref.shape[1]
    lats = hemisphere // half_bands
    total_lat = 2 * hemisphere
    fields, vectors = even_ref.shape[2], even_ref.shape[1]
    own = wlist_ref[lax.axis_index("band")]
    ri = lax.broadcasted_iota(jnp.int32, (128, 128), 0)
    ci = lax.broadcasted_iota(jnp.int32, (128, 128), 1)
    mirror = jnp.where(ri + ci == lats - 1, 1.0, 0.0).astype(BF16)
    south = rows_ref[half_bands:].reshape(half_bands * depth, 128)
    south = lax.dot_general(south, mirror, NN, preferred_element_type=F32)
    for b in range(half_bands):
        north_b = rows_ref[b].astype(F32)
        s = half_bands - 1 - b
        south_b = south[s * depth : (s + 1) * depth]
        fold[0, :, lats * b : lats * (b + 1)] = (north_b + south_b)[:, :lats]
        fold[1, :, lats * b : lats * (b + 1)] = (north_b - south_b)[:, :lats]
    sym, anti = fold[0].astype(BF16), fold[1].astype(BF16)
    even_all = lax.dot_general(sym, even_t_ref[0], NT, preferred_element_type=F32)
    odd_all = lax.dot_general(anti, odd_ref[0], NN, preferred_element_type=F32)
    half = depth // 2
    even_col = lax.broadcasted_iota(jnp.int32, (half, hemisphere + 1), 1)
    odd_col = lax.broadcasted_iota(jnp.int32, (half, hemisphere), 1)
    even = jnp.where(even_col < (total_lat + 1 - own) // 2, even_all[:half], even_all[half:])
    odd = jnp.where(odd_col < (total_lat - own) // 2, odd_all[:half], odd_all[half:])
    parts = fields * 2
    for fr in range(parts):
        for v in range(vectors):
            f, r, place = fr // 2, fr % 2, fr * vectors + v
            even_ref[0, v, f, r : r + 1, :] = even[place : place + 1]
            odd_out_ref[0, v, f, r : r + 1, :] = odd[place : place + 1]
    tiles = hemisphere // 128
    first = lax.broadcasted_iota(jnp.int32, (8, 128), 0) < vectors
    corner = (lax.broadcasted_iota(jnp.int32, (8, 128), 1) == 0) & first
    for fr in range(parts):
        base = fr // 2 * 8
        for i in range(tiles):
            ev = even[base : base + 8, 128 * i : 128 * (i + 1)]
            od = odd[base : base + 8, 128 * i : 128 * (i + 1)]
            if fr % 2 == 0:
                tile = jnp.where(first, ev, pltpu.roll(od, 4, 0))
            else:
                tile = jnp.where(first, pltpu.roll(ev, 4, 0), od)
            send_ref[fr * tiles + i] = tile.astype(BF16)
        last = jnp.broadcast_to(even[base : base + 8, hemisphere : hemisphere + 1], (8, 128))
        if fr % 2 == 1:
            last = pltpu.roll(last, 4, 0)
        send_ref[parts * tiles + fr] = jnp.where(corner, last, 0.0).astype(BF16)
    for t in range(parts * (tiles + 1), send_ref.shape[0]):
        send_ref[t] = jnp.zeros((8, 128), BF16)


def gram_kernel(tiles_ref, out_ref):
    count = tiles_ref.shape[0]
    pairs = tiles_ref[...].astype(F32).reshape(count // 2, 2, 8, 128)
    low, high = pairs[:, 0], pairs[:, 1]
    first = lax.broadcasted_iota(jnp.int32, low.shape, 1) < 4
    even = jnp.where(first, low, pltpu.roll(high, 4, 1)).reshape(4 * count, 128).astype(BF16)
    odd = jnp.where(first, pltpu.roll(low, 4, 1), high).reshape(4 * count, 128).astype(BF16)
    gram = lax.dot_general(even, even, NT, preferred_element_type=F32)
    gram = gram + lax.dot_general(odd, odd, NT, preferred_element_type=F32)
    for t in range(count):
        out_ref[t] = gram[4 * t : 4 * t + 4]


def spread_kernel(parts_ref, out_ref):
    total = jnp.sum(parts_ref[...], axis=0)
    out_ref[...] = jnp.broadcast_to(total[None], out_ref.shape)


def on_device(grid, trunc, wlist, leg_even, leg_odd):
    bands = lax.axis_size("band")
    tans = lax.axis_size("tan")
    vectors, fields, lats, lons = grid.shape
    total_lat = lats * bands
    depth = 4 * vectors * fields
    vmem = pl.BlockSpec(memory_space=pltpu.VMEM)
    smem = pl.BlockSpec(memory_space=pltpu.SMEM)
    params = pltpu.CompilerParams(vmem_limit_bytes=32 * 1024 * 1024)

    lat_rows = pl.pallas_call(
        fourier_kernel,
        name="fourier",
        out_shape=jax.ShapeDtypeStruct((bands, depth, 128), BF16),
        in_specs=[smem, vmem, vmem],
        out_specs=vmem,
        scratch_shapes=[pltpu.VMEM((4 * bands, lons), BF16), pltpu.VMEM((bands * depth, 128), F32)],
        compiler_params=params,
    )(wlist, trunc.reshape(1, lats), grid)
    received = lax.all_to_all(lat_rows, "band", split_axis=0, concat_axis=0, tiled=True)

    even, odd, tiles = pl.pallas_call(
        legendre_kernel,
        name="legendre",
        out_shape=(
            jax.ShapeDtypeStruct((1, vectors, fields, 2, leg_even.shape[2]), F32),
            jax.ShapeDtypeStruct((1, vectors, fields, 2, leg_odd.shape[2]), F32),
            jax.ShapeDtypeStruct((tans, 2 * vectors, 128), BF16),
        ),
        in_specs=[smem, vmem, vmem, vmem],
        out_specs=(vmem, vmem, vmem),
        scratch_shapes=[pltpu.VMEM((2, depth, total_lat // 2), F32)],
        compiler_params=params,
    )(wlist, received, jnp.swapaxes(leg_even, 1, 2), leg_odd)
    tiles = lax.all_to_all(tiles, "tan", split_axis=0, concat_axis=0, tiled=True)

    products = pl.pallas_call(
        gram_kernel,
        name="gram",
        out_shape=jax.ShapeDtypeStruct((tans, vectors, vectors * tans), F32),
        in_specs=[vmem],
        out_specs=vmem,
        compiler_params=params,
    )(tiles)
    products = lax.all_to_all(products, "tan", split_axis=0, concat_axis=0, tiled=True)

    spread = pl.pallas_call(
        spread_kernel,
        name="spread",
        out_shape=jax.ShapeDtypeStruct((bands, vectors, vectors * tans), F32),
        in_specs=[vmem],
        out_specs=vmem,
        compiler_params=params,
    )(products)
    summed = lax.all_to_all(spread, "band", split_axis=0, concat_axis=0, tiled=True)
    inner = jnp.sum(summed, axis=0).T / (bands * 4.0 * (total_lat + 1))
    return (even, odd, inner)


def solution(mesh):
    return jax.shard_map(
        on_device,
        mesh=mesh,
        in_specs=(
            P("tan", None, "band", None),
            P("band"),
            P(),
            P("band", None, None),
            P("band", None, None),
        ),
        out_specs=(
            P("band", "tan", None, None, None),
            P("band", "tan", None, None, None),
            P(None, "tan"),
        ),
        check_vma=False,
    )
```

```python
import functools
import math

import jax
import jax.numpy as jnp
from jax import lax
from jax.experimental import pallas as pl
from jax.experimental.pallas import tpu as pltpu
from jax.sharding import PartitionSpec as P

F32 = jnp.float32
BF16 = jnp.bfloat16
NT = (((1,), (1,)), ((), ()))
NN = (((1,), (0,)), ((), ()))


def fourier_kernel(wlist_hbm, trunc_hbm, grid_hbm, out_ref, wlist_ref, trunc_ref, grid_ref, table, rows, small, sems):
    vectors, fields, lats, lons = grid_ref.shape
    bands = wlist_ref.shape[0]
    total_lat = lats * bands
    members = 2 * bands
    get_wlist = pltpu.make_async_copy(wlist_hbm, wlist_ref, small.at[0])
    get_trunc = pltpu.make_async_copy(trunc_hbm, trunc_ref, small.at[1])
    get_wlist.start()
    get_trunc.start()
    places = [(v, f) for v in range(vectors) for f in range(fields)]
    fetches = [
        pltpu.make_async_copy(grid_hbm.at[v, f], grid_ref.at[v, f], sems.at[n])
        for n, (v, f) in enumerate(places)
    ]
    for fetch in fetches:
        fetch.start()
    row = lax.broadcasted_iota(jnp.int32, (members, 128), 0)
    lane = lax.broadcasted_iota(jnp.int32, (members, 128), 1)
    get_wlist.wait()
    mvals = jnp.zeros((members, 128), jnp.int32)
    for b in range(bands):
        wave = wlist_ref[b]
        mvals = jnp.where(row == b, wave, mvals)
        mvals = jnp.where(row == bands + b, total_lat - 1 - wave, mvals)
    unit = 2.0 * math.pi / lons
    scaling = 1.0 / math.sqrt(lons)
    chunks = lons // 128
    fine = (mvals * lane % lons).astype(F32) * unit
    coarse = (mvals * lane % chunks).astype(F32) * (128.0 * unit)
    fine_cos, fine_sin = jnp.cos(fine), jnp.sin(fine)
    coarse_cos, coarse_sin = jnp.cos(coarse) * scaling, jnp.sin(coarse) * scaling
    for i in range(chunks):
        cc, cs = coarse_cos[:, i : i + 1], coarse_sin[:, i : i + 1]
        table[:members, 128 * i : 128 * (i + 1)] = (cc * fine_cos - cs * fine_sin).astype(BF16)
        table[members:, 128 * i : 128 * (i + 1)] = (-(cs * fine_cos + cc * fine_sin)).astype(BF16)
    get_trunc.wait()
    keep = mvals[:, :lats] <= trunc_ref[...]
    keep = jnp.concatenate([keep, keep], axis=0)
    depth = 4 * vectors * fields
    for n, (v, f) in enumerate(places):
        fetches[n].wait()
        spectra = lax.dot_general(table[...], grid_ref[v, f], NT, preferred_element_type=F32)
        spectra = jnp.where(keep, spectra, 0.0)
        spectra = jnp.pad(spectra, ((0, 0), (0, 128 - lats)))
        for r in range(2):
            for p in range(2):
                place = ((p * fields + f) * 2 + r) * vectors + v
                start = (r * 2 + p) * bands
                rows[pl.ds(place, bands, stride=depth), :] = spectra[start : start + bands]
    out_ref[...] = rows[...].astype(BF16).reshape(out_ref.shape)


def legendre_kernel(wlist_ref, rows_ref, even_t_ref, odd_ref, even_ref, odd_out_ref, send_ref, fold):
    bands, depth, _ = rows_ref.shape
    half_bands = bands // 2
    hemisphere = odd_ref.shape[1]
    lats = hemisphere // half_bands
    total_lat = 2 * hemisphere
    fields, vectors = even_ref.shape[2], even_ref.shape[1]
    own = wlist_ref[lax.axis_index("band")]
    ri = lax.broadcasted_iota(jnp.int32, (128, 128), 0)
    ci = lax.broadcasted_iota(jnp.int32, (128, 128), 1)
    mirror = jnp.where(ri + ci == lats - 1, 1.0, 0.0).astype(BF16)
    south = rows_ref[half_bands:].reshape(half_bands * depth, 128)
    south = lax.dot_general(south, mirror, NN, preferred_element_type=F32)
    for b in range(half_bands):
        north_b = rows_ref[b].astype(F32)
        s = half_bands - 1 - b
        south_b = south[s * depth : (s + 1) * depth]
        fold[0, :, lats * b : lats * (b + 1)] = (north_b + south_b)[:, :lats]
        fold[1, :, lats * b : lats * (b + 1)] = (north_b - south_b)[:, :lats]
    sym, anti = fold[0].astype(BF16), fold[1].astype(BF16)
    even_all = lax.dot_general(sym, even_t_ref[0], NT, preferred_element_type=F32)
    odd_all = lax.dot_general(anti, odd_ref[0], NN, preferred_element_type=F32)
    half = depth // 2
    even_col = lax.broadcasted_iota(jnp.int32, (half, hemisphere + 1), 1)
    odd_col = lax.broadcasted_iota(jnp.int32, (half, hemisphere), 1)
    even = jnp.where(even_col < (total_lat + 1 - own) // 2, even_all[:half], even_all[half:])
    odd = jnp.where(odd_col < (total_lat - own) // 2, odd_all[:half], odd_all[half:])
    parts = fields * 2
    for fr in range(parts):
        for v in range(vectors):
            f, r, place = fr // 2, fr % 2, fr * vectors + v
            even_ref[0, v, f, r : r + 1, :] = even[place : place + 1]
            odd_out_ref[0, v, f, r : r + 1, :] = odd[place : place + 1]
    columns = send_ref.shape[0] // parts
    tiles = hemisphere // 128
    first = lax.broadcasted_iota(jnp.int32, (8, 128), 0) < vectors
    corner = (lax.broadcasted_iota(jnp.int32, (8, 128), 1) == 0) & first
    for fr in range(parts):
        base = fr // 2 * 8
        for i in range(tiles):
            ev = even[base : base + 8, 128 * i : 128 * (i + 1)]
            od = odd[base : base + 8, 128 * i : 128 * (i + 1)]
            if fr % 2 == 0:
                tile = jnp.where(first, ev, pltpu.roll(od, 4, 0))
            else:
                tile = jnp.where(first, pltpu.roll(ev, 4, 0), od)
            tile = tile.astype(BF16)
            for z in range(columns):
                send_ref[fr * columns + z, i] = tile
        last = jnp.broadcast_to(even[base : base + 8, hemisphere : hemisphere + 1], (8, 128))
        if fr % 2 == 1:
            last = pltpu.roll(last, 4, 0)
        last = jnp.where(corner, last, 0.0).astype(BF16)
        for z in range(columns):
            send_ref[fr * columns + z, tiles] = last


def gram_kernel(columns, tiles_ref, out_ref, gram_ref):
    count, tiles = tiles_ref.shape[:2]
    peers = out_ref.shape[0]
    wide = count // columns
    first = lax.broadcasted_iota(jnp.int32, (count // 2, 8, 128), 1) < 4
    evens, odds = [], []
    for i in range(tiles):
        pairs = tiles_ref[:, i].astype(F32).reshape(count // 2, 2, 8, 128)
        low, high = pairs[:, 0], pairs[:, 1]
        evens.append(jnp.where(first, low, pltpu.roll(high, 4, 1)).reshape(4 * count, 128).astype(BF16))
        if i < tiles - 1:
            odds.append(jnp.where(first, pltpu.roll(low, 4, 1), high).reshape(4 * count, 128).astype(BF16))
    both = jnp.concatenate(evens + odds, axis=1)
    gram = lax.dot_general(both, both, NT, preferred_element_type=F32)
    for t in range(count):
        gram_ref[t] = gram[4 * t : 4 * t + 4]
    z = lax.axis_index("z")
    for x in range(wide):
        block = gram_ref[x * columns + z].astype(BF16)
        for b in range(peers // wide):
            out_ref[b * wide + x] = block


def sum_kernel(scale, parts_ref, out_ref):
    out_ref[...] = jnp.sum(parts_ref[...].astype(F32), axis=0) * scale


def on_device(grid, trunc, wlist, leg_even, leg_odd):
    bands = lax.axis_size("band")
    tans = lax.axis_size(("x", "z"))
    vectors, fields, lats, lons = grid.shape
    total_lat = lats * bands
    depth = 4 * vectors * fields
    vmem = pl.BlockSpec(memory_space=pltpu.VMEM)
    smem = pl.BlockSpec(memory_space=pltpu.SMEM)
    params = pltpu.CompilerParams(vmem_limit_bytes=32 * 1024 * 1024)

    hbm = pl.BlockSpec(memory_space=pltpu.HBM)
    lat_rows = pl.pallas_call(
        fourier_kernel,
        name="fourier",
        out_shape=jax.ShapeDtypeStruct((bands, depth, 128), BF16),
        in_specs=[hbm, hbm, hbm],
        out_specs=vmem,
        scratch_shapes=[
            pltpu.SMEM((bands,), jnp.int32),
            pltpu.VMEM((1, lats), jnp.int32),
            pltpu.VMEM(grid.shape, BF16),
            pltpu.VMEM((4 * bands, lons), BF16),
            pltpu.VMEM((bands * depth, 128), F32),
            pltpu.SemaphoreType.DMA((2,)),
            pltpu.SemaphoreType.DMA((vectors * fields,)),
        ],
        compiler_params=params,
    )(
        pltpu.with_memory_space_constraint(wlist, pltpu.HBM),
        pltpu.with_memory_space_constraint(trunc.reshape(1, lats), pltpu.HBM),
        pltpu.with_memory_space_constraint(grid, pltpu.HBM),
    )
    received = lax.all_to_all(lat_rows, "band", split_axis=0, concat_axis=0, tiled=True)

    even, odd, tiles = pl.pallas_call(
        legendre_kernel,
        name="legendre",
        out_shape=(
            jax.ShapeDtypeStruct((1, vectors, fields, 2, leg_even.shape[2]), F32),
            jax.ShapeDtypeStruct((1, vectors, fields, 2, leg_odd.shape[2]), F32),
            jax.ShapeDtypeStruct((tans, total_lat // 256 + 1, 2 * vectors, 128), BF16),
        ),
        in_specs=[smem, vmem, vmem, vmem],
        out_specs=(vmem, vmem, vmem),
        scratch_shapes=[pltpu.VMEM((2, depth, total_lat // 2), F32)],
        compiler_params=params,
    )(wlist, received, jnp.swapaxes(leg_even, 1, 2), leg_odd)
    tiles = lax.all_to_all(tiles, ("x", "z"), split_axis=0, concat_axis=0, tiled=True)

    parts = 2 * fields
    columns = tans // parts
    products = pl.pallas_call(
        functools.partial(gram_kernel, columns),
        name="gram",
        out_shape=jax.ShapeDtypeStruct((bands * parts, vectors, vectors * tans), BF16),
        in_specs=[vmem],
        out_specs=vmem,
        scratch_shapes=[pltpu.VMEM((tans, vectors, vectors * tans), F32)],
        compiler_params=params,
    )(tiles)
    products = lax.all_to_all(products, ("band", "x"), split_axis=0, concat_axis=0, tiled=True)

    scale = 1.0 / (bands * 4.0 * (total_lat + 1))
    inner = pl.pallas_call(
        functools.partial(sum_kernel, scale),
        name="sum",
        out_shape=jax.ShapeDtypeStruct((vectors, vectors * tans), F32),
        in_specs=[vmem],
        out_specs=vmem,
        compiler_params=params,
    )(products)
    return (even, odd, inner.T)


def solution(mesh):
    bands, tans = mesh.devices.shape
    split = jax.sharding.Mesh(mesh.devices.reshape(bands, 4, tans // 4), ("band", "x", "z"))
    tan = ("x", "z")
    return jax.shard_map(
        on_device,
        mesh=split,
        in_specs=(
            P(tan, None, "band", None),
            P("band"),
            P(),
            P("band", None, None),
            P("band", None, None),
        ),
        out_specs=(
            P("band", tan, None, None, None),
            P("band", tan, None, None, None),
            P(None, tan),
        ),
        check_vma=False,
    )
```

```python
import functools
import math

import jax
import jax.numpy as jnp
from jax import lax
from jax.experimental import pallas as pl
from jax.experimental.pallas import tpu as pltpu
from jax.sharding import PartitionSpec as P

F32 = jnp.float32
BF16 = jnp.bfloat16
NT = (((1,), (1,)), ((), ()))
NN = (((1,), (0,)), ((), ()))


def fourier_kernel(wlist_hbm, trunc_hbm, grid_hbm, out_ref, own_ref, wlist_ref, trunc_ref, grid_ref, table, rows, small, sems):
    vectors, fields, lats, lons = grid_ref.shape
    bands = wlist_ref.shape[0]
    total_lat = lats * bands
    members = 2 * bands
    get_wlist = pltpu.make_async_copy(wlist_hbm, wlist_ref, small.at[0])
    get_trunc = pltpu.make_async_copy(trunc_hbm, trunc_ref, small.at[1])
    get_wlist.start()
    get_trunc.start()
    half = vectors // 2
    fetches = [
        pltpu.make_async_copy(grid_hbm.at[pl.ds(v, half)], grid_ref.at[pl.ds(v, half)], sems.at[n])
        for n, v in enumerate(range(0, vectors, half))
    ]
    for fetch in fetches:
        fetch.start()
    row = lax.broadcasted_iota(jnp.int32, (members, 128), 0)
    lane = lax.broadcasted_iota(jnp.int32, (members, 128), 1)
    get_wlist.wait()
    mvals = jnp.zeros((members, 128), jnp.int32)
    for b in range(bands):
        wave, place = wlist_ref[b], b
        mvals = jnp.where(row == place, wave, mvals)
        mvals = jnp.where(row == bands + place, total_lat - 1 - wave, mvals)
    own_ref[...] = jnp.full(own_ref.shape, wlist_ref[lax.axis_index("band")], jnp.int32)
    unit = 2.0 * math.pi / lons
    scaling = 1.0 / math.sqrt(lons)
    chunks = lons // 128
    fine = (mvals * lane % lons).astype(F32) * unit
    coarse = (mvals * lane % chunks).astype(F32) * (128.0 * unit)
    fine_cos, fine_sin = jnp.cos(fine), jnp.sin(fine)
    coarse_cos, coarse_sin = jnp.cos(coarse) * scaling, jnp.sin(coarse) * scaling
    for i in range(chunks):
        cc, cs = coarse_cos[:, i : i + 1], coarse_sin[:, i : i + 1]
        table[:members, 128 * i : 128 * (i + 1)] = (cc * fine_cos - cs * fine_sin).astype(BF16)
        table[members:, 128 * i : 128 * (i + 1)] = (-(cs * fine_cos + cc * fine_sin)).astype(BF16)
    get_trunc.wait()
    keep = mvals[:, :lats] <= trunc_ref[...]
    keep = jnp.concatenate([keep, keep], axis=0)
    depth = 4 * vectors * fields
    for v in range(vectors):
        if v % half == 0:
            fetches[v // half].wait()
        for f in range(fields):
            spectra = lax.dot_general(table[...], grid_ref[v, f], NT, preferred_element_type=F32)
            spectra = jnp.where(keep, spectra, 0.0)
            spectra = jnp.pad(spectra, ((0, 0), (0, 128 - lats)))
            for r in range(2):
                for p in range(2):
                    place = ((p * fields + f) * 2 + r) * vectors + v
                    start = (r * 2 + p) * bands
                    rows[pl.ds(place, bands, stride=depth), :] = spectra[start : start + bands]
    out_ref[...] = rows[...].astype(BF16).reshape(out_ref.shape)


def legendre_kernel(own_ref, rows_ref, even_t_ref, odd_ref, send_ref, even_ref, odd_out_ref, fold):
    bands, depth, _ = rows_ref.shape
    half_bands = bands // 2
    hemisphere = odd_ref.shape[1]
    lats = hemisphere // half_bands
    total_lat = 2 * hemisphere
    own = own_ref[0:1, 0:1]
    ri = lax.broadcasted_iota(jnp.int32, (128, 128), 0)
    ci = lax.broadcasted_iota(jnp.int32, (128, 128), 1)
    mirror = jnp.where(ri + ci == lats - 1, 1.0, 0.0).astype(BF16)
    south = rows_ref[half_bands:].reshape(half_bands * depth, 128)
    south = lax.dot_general(south, mirror, NN, preferred_element_type=F32)
    for b in range(half_bands):
        north_b = rows_ref[b].astype(F32)
        s = half_bands - 1 - b
        south_b = south[s * depth : (s + 1) * depth]
        fold[0, :, lats * b : lats * (b + 1)] = (north_b + south_b)[:, :lats]
        fold[1, :, lats * b : lats * (b + 1)] = (north_b - south_b)[:, :lats]
    sym, anti = fold[0].astype(BF16), fold[1].astype(BF16)
    even_all = lax.dot_general(sym, even_t_ref[0], NT, preferred_element_type=F32)
    odd_all = lax.dot_general(anti, odd_ref[0], NN, preferred_element_type=F32)
    half = depth // 2
    even_col = lax.broadcasted_iota(jnp.int32, (half, hemisphere + 1), 1)
    odd_col = lax.broadcasted_iota(jnp.int32, (half, hemisphere), 1)
    even = jnp.where(even_col < ((total_lat + 1 - own) >> 1), even_all[:half], even_all[half:])
    odd = jnp.where(odd_col < ((total_lat - own) >> 1), odd_all[:half], odd_all[half:])
    even_ref[...] = even
    odd_out_ref[...] = odd
    tiles = hemisphere // 128
    vectors = 4
    parts = half // vectors
    columns = 2 * send_ref.shape[0] // parts
    last = jnp.broadcast_to(even[:, hemisphere : hemisphere + 1], (half, 128))
    last = jnp.where(lax.broadcasted_iota(jnp.int32, (half, 128), 1) == 0, last, 0.0)
    pieces = [even[:, 128 * i : 128 * (i + 1)] for i in range(tiles)]
    pieces += [odd[:, 128 * i : 128 * (i + 1)] for i in range(tiles)]
    pieces += [last]
    first = lax.broadcasted_iota(jnp.int32, (8, 128), 0) < vectors
    for fr in range(parts):
        base = fr // 2 * 8
        same = [piece[base : base + 8] for piece in pieces]
        other = [pltpu.roll(piece, vectors, 0) for piece in same]
        low, high = (same, other) if fr % 2 == 0 else (other, same)
        quarters = 2 * list(range(len(pieces)))
        slab = [jnp.where(first, low[i], high[j]) for i, j in zip(quarters[0::2], quarters[1::2])]
        slab = jnp.concatenate(slab, axis=0).astype(BF16)
        for pair in range(columns // 2):
            send_ref[fr * columns // 2 + pair] = slab


def gram_kernel(columns, tiles_ref, out_ref, gram_ref):
    pairs, depth, _ = tiles_ref.shape
    vectors = 4
    count, tiles = 2 * pairs, depth // (2 * vectors)
    wide = count // columns
    slabs = tiles_ref[...].astype(F32)
    eights = [slabs[:, 8 * k : 8 * (k + 1)] for k in range(tiles)]
    first = lax.broadcasted_iota(jnp.int32, (pairs, 8, 128), 1) < vectors
    half = tiles // 2
    columns_of = []
    for i in range(tiles):
        if i % 2 == 0:
            both = jnp.where(first, eights[i // 2], eights[half + i // 2])
        else:
            both = jnp.where(first, eights[half + (i + 1) // 2], eights[i // 2])
            both = pltpu.roll(both, vectors, 1)
        columns_of.append(both.reshape(count * vectors, 128).astype(BF16))
    both = jnp.concatenate(columns_of, axis=1)
    gram = lax.dot_general(both, both, NT, preferred_element_type=F32)
    gram_ref[...] = gram.reshape(gram_ref.shape)
    z = lax.axis_index("z")
    rows = [gram_ref[x, lax.div(z, 2)] for x in range(wide)]
    rows = [jnp.where(lax.rem(z, 2) == 0, row, pltpu.roll(row, vectors, 0)) for row in rows]
    first = lax.broadcasted_iota(jnp.int32, (8, 128), 0) < vectors
    rows = [jnp.where(first, rows[x], pltpu.roll(rows[x + 1], vectors, 0)) for x in range(0, wide, 2)]
    block = jnp.concatenate(rows, axis=0).astype(BF16)
    for b in range(out_ref.shape[0]):
        out_ref[b] = block


def finish_kernel(scale, parts_ref, even_in_ref, odd_in_ref, inner_ref, even_ref, odd_ref):
    _, vectors, fields, parts, _ = even_ref.shape
    for f in range(fields):
        for r in range(parts):
            for v in range(vectors):
                row = (f * parts + r) * vectors + v
                even_ref[0, v, f, r : r + 1, :] = even_in_ref[row : row + 1]
                odd_ref[0, v, f, r : r + 1, :] = odd_in_ref[row : row + 1]
    total = jnp.sum(parts_ref[...].astype(F32), axis=0)
    inner_ref[...] = (total[:vectors] + total[vectors:]) * scale


VMEM = pl.BlockSpec(memory_space=pltpu.VMEM)
HBM = pl.BlockSpec(memory_space=pltpu.HBM)
PARAMS = pltpu.CompilerParams(vmem_limit_bytes=32 * 1024 * 1024)


def in_hbm(array):
    return pltpu.with_memory_space_constraint(array, pltpu.HBM)


def fourier(wlist, trunc, grid):
    vectors, fields, lats, lons = grid.shape
    bands = wlist.shape[0]
    depth = 4 * vectors * fields
    return pl.pallas_call(
        fourier_kernel,
        name="fourier",
        out_shape=(
            jax.ShapeDtypeStruct((bands, depth, 128), BF16),
            jax.ShapeDtypeStruct((8, 128), jnp.int32),
        ),
        in_specs=[HBM, HBM, HBM],
        out_specs=(VMEM, VMEM),
        scratch_shapes=[
            pltpu.SMEM((bands,), jnp.int32),
            pltpu.VMEM((1, lats), jnp.int32),
            pltpu.VMEM(grid.shape, BF16),
            pltpu.VMEM((4 * bands, lons), BF16),
            pltpu.VMEM((bands * depth, 128), F32),
            pltpu.SemaphoreType.DMA((2,)),
            pltpu.SemaphoreType.DMA((2,)),
        ],
        compiler_params=PARAMS,
    )(in_hbm(wlist), in_hbm(trunc.reshape(1, lats)), in_hbm(grid))


def legendre(own, received, leg_even, leg_odd, vectors, tans):
    depth = received.shape[1]
    hemisphere = leg_odd.shape[2]
    return pl.pallas_call(
        legendre_kernel,
        name="legendre",
        out_shape=(
            jax.ShapeDtypeStruct((tans // 2, 2 * (hemisphere // 64 + 1) * vectors, 128), BF16),
            jax.ShapeDtypeStruct((depth // 2, leg_even.shape[2]), F32),
            jax.ShapeDtypeStruct((depth // 2, leg_odd.shape[2]), F32),
        ),
        in_specs=[VMEM] * 4,
        out_specs=(VMEM, VMEM, VMEM),
        scratch_shapes=[pltpu.VMEM((2, depth, hemisphere), F32)],
        compiler_params=PARAMS,
    )(own, received, jnp.swapaxes(leg_even, 1, 2), leg_odd)


def gram(tiles, columns, bands, vectors):
    tans = 2 * tiles.shape[0]
    wide = tans // columns
    return pl.pallas_call(
        functools.partial(gram_kernel, columns),
        name="gram",
        out_shape=jax.ShapeDtypeStruct((bands, wide * vectors, vectors * tans), BF16),
        in_specs=[VMEM],
        out_specs=VMEM,
        scratch_shapes=[pltpu.VMEM((wide, columns // 2, 2 * vectors, vectors * tans), F32)],
        compiler_params=PARAMS,
    )(tiles)


def finish(products, even, odd, scale, vectors, fields):
    return pl.pallas_call(
        functools.partial(finish_kernel, scale),
        name="finish",
        out_shape=(
            jax.ShapeDtypeStruct((vectors, products.shape[2]), F32),
            jax.ShapeDtypeStruct((1, vectors, fields, 2, even.shape[1]), F32),
            jax.ShapeDtypeStruct((1, vectors, fields, 2, odd.shape[1]), F32),
        ),
        in_specs=[VMEM] * 3,
        out_specs=(VMEM, VMEM, VMEM),
        compiler_params=PARAMS,
    )(products, even, odd)


def on_device(grid, trunc, wlist, leg_even, leg_odd):
    bands = lax.axis_size("band")
    columns = lax.axis_size("z")
    tans = lax.axis_size(("x", "z"))
    vectors, fields, lats, _ = grid.shape
    total_lat = lats * bands
    lat_rows, own = fourier(wlist, trunc, grid)
    received = lax.all_to_all(lat_rows, "band", 0, 0, tiled=True)
    tiles, even, odd = legendre(own, received, leg_even, leg_odd, vectors, tans)
    slab = tiles.shape
    tiles = tiles.reshape(tans, slab[1] // (2 * vectors), vectors, 128)
    tiles = lax.all_to_all(tiles, ("x", "z"), split_axis=0, concat_axis=0, tiled=True)
    products = gram(tiles.reshape(slab), columns, bands, vectors)
    products = products.reshape(-1, vectors, vectors * tans)
    products = lax.all_to_all(products, ("band", "x"), split_axis=0, concat_axis=0, tiled=True)
    products = products.reshape(-1, 2 * vectors, vectors * tans)
    scale = 1.0 / (bands * 4.0 * (total_lat + 1))
    inner, even, odd = finish(products, even, odd, scale, vectors, fields)
    return (even, odd, inner.T)


def solution(mesh):
    bands, tans = mesh.devices.shape
    split = jax.sharding.Mesh(mesh.devices.reshape(bands, 4, tans // 4), ("band", "x", "z"))
    tan = ("x", "z")
    return jax.shard_map(
        on_device,
        mesh=split,
        in_specs=(
            P(tan, None, "band", None),
            P("band"),
            P(),
            P("band", None, None),
            P("band", None, None),
        ),
        out_specs=(
            P("band", tan, None, None, None),
            P("band", tan, None, None, None),
            P(None, tan),
        ),
        check_vma=False,
    )
```

```python
import functools
import math

import jax
import jax.numpy as jnp
from jax import lax
from jax.experimental import pallas as pl
from jax.experimental.pallas import tpu as pltpu
from jax.sharding import PartitionSpec as P

F32 = jnp.float32
FIRST_BAND, FIRST_X, FIRST_Z = 13, 2, 6
BF16 = jnp.bfloat16
NT = (((1,), (1,)), ((), ()))
NN = (((1,), (0,)), ((), ()))


def turned(count, first):
    return [(first + n) % count for n in range(count)]


def fourier_kernel(wlist_hbm, trunc_hbm, grid_hbm, out_ref, own_ref, wlist_ref, trunc_ref, grid_ref, table, rows, small, sems):
    vectors, fields, lats, lons = grid_ref.shape
    bands = wlist_ref.shape[0]
    total_lat = lats * bands
    members = 2 * bands
    get_wlist = pltpu.make_async_copy(wlist_hbm, wlist_ref, small.at[0])
    get_trunc = pltpu.make_async_copy(trunc_hbm, trunc_ref, small.at[1])
    get_wlist.start()
    get_trunc.start()
    half = vectors // 2
    fetches = [
        pltpu.make_async_copy(grid_hbm.at[pl.ds(v, half)], grid_ref.at[pl.ds(v, half)], sems.at[n])
        for n, v in enumerate(range(0, vectors, half))
    ]
    for fetch in fetches:
        fetch.start()
    row = lax.broadcasted_iota(jnp.int32, (members, 128), 0)
    lane = lax.broadcasted_iota(jnp.int32, (members, 128), 1)
    get_wlist.wait()
    mvals = jnp.zeros((members, 128), jnp.int32)
    for b in range(bands):
        wave, place = wlist_ref[b], (b - FIRST_BAND) % bands
        mvals = jnp.where(row == place, wave, mvals)
        mvals = jnp.where(row == bands + place, total_lat - 1 - wave, mvals)
    own_ref[...] = jnp.full(own_ref.shape, wlist_ref[lax.axis_index("band")], jnp.int32)
    unit = 2.0 * math.pi / lons
    scaling = 1.0 / math.sqrt(lons)
    chunks = lons // 128
    fine = (mvals * lane % lons).astype(F32) * unit
    coarse = (mvals * lane % chunks).astype(F32) * (128.0 * unit)
    fine_cos, fine_sin = jnp.cos(fine), jnp.sin(fine)
    coarse_cos, coarse_sin = jnp.cos(coarse) * scaling, jnp.sin(coarse) * scaling
    for i in range(chunks):
        cc, cs = coarse_cos[:, i : i + 1], coarse_sin[:, i : i + 1]
        table[:members, 128 * i : 128 * (i + 1)] = (cc * fine_cos - cs * fine_sin).astype(BF16)
        table[members:, 128 * i : 128 * (i + 1)] = (-(cs * fine_cos + cc * fine_sin)).astype(BF16)
    get_trunc.wait()
    keep = mvals[:, :lats] <= trunc_ref[...]
    keep = jnp.concatenate([keep, keep], axis=0)
    depth = 4 * vectors * fields
    for v in range(vectors):
        if v % half == 0:
            fetches[v // half].wait()
        for f in range(fields):
            spectra = lax.dot_general(table[...], grid_ref[v, f], NT, preferred_element_type=F32)
            spectra = jnp.where(keep, spectra, 0.0)
            spectra = jnp.pad(spectra, ((0, 0), (0, 128 - lats)))
            for r in range(2):
                for p in range(2):
                    place = ((p * fields + f) * 2 + r) * vectors + v
                    start = (r * 2 + p) * bands
                    rows[pl.ds(place, bands, stride=depth), :] = spectra[start : start + bands]
    out_ref[...] = rows[...].astype(BF16).reshape(out_ref.shape)


def legendre_kernel(own_ref, rows_ref, even_t_ref, odd_ref, send_ref, even_ref, odd_out_ref, fold):
    bands, depth, _ = rows_ref.shape
    half_bands = bands // 2
    hemisphere = odd_ref.shape[1]
    lats = hemisphere // half_bands
    total_lat = 2 * hemisphere
    own = own_ref[0:1, 0:1]
    ri = lax.broadcasted_iota(jnp.int32, (128, 128), 0)
    ci = lax.broadcasted_iota(jnp.int32, (128, 128), 1)
    mirror = jnp.where(ri + ci == lats - 1, 1.0, 0.0).astype(BF16)
    south = [rows_ref[(b - FIRST_BAND) % bands] for b in range(half_bands, bands)]
    south = jnp.concatenate(south, axis=0)
    south = lax.dot_general(south, mirror, NN, preferred_element_type=F32)
    for b in range(half_bands):
        north_b = rows_ref[(b - FIRST_BAND) % bands].astype(F32)
        s = half_bands - 1 - b
        south_b = south[s * depth : (s + 1) * depth]
        fold[0, :, lats * b : lats * (b + 1)] = (north_b + south_b)[:, :lats]
        fold[1, :, lats * b : lats * (b + 1)] = (north_b - south_b)[:, :lats]
    sym, anti = fold[0].astype(BF16), fold[1].astype(BF16)
    even_all = lax.dot_general(sym, even_t_ref[0], NT, preferred_element_type=F32)
    odd_all = lax.dot_general(anti, odd_ref[0], NN, preferred_element_type=F32)
    half = depth // 2
    even_col = lax.broadcasted_iota(jnp.int32, (half, hemisphere + 1), 1)
    odd_col = lax.broadcasted_iota(jnp.int32, (half, hemisphere), 1)
    even = jnp.where(even_col < ((total_lat + 1 - own) >> 1), even_all[:half], even_all[half:])
    odd = jnp.where(odd_col < ((total_lat - own) >> 1), odd_all[:half], odd_all[half:])
    even_ref[...] = even
    odd_out_ref[...] = odd
    tiles = hemisphere // 128
    vectors = 4
    parts = half // vectors
    columns = 2 * send_ref.shape[0] // parts
    last = jnp.broadcast_to(even[:, hemisphere : hemisphere + 1], (half, 128))
    last = jnp.where(lax.broadcasted_iota(jnp.int32, (half, 128), 1) == 0, last, 0.0)
    pieces = [even[:, 128 * i : 128 * (i + 1)] for i in range(tiles)]
    pieces += [odd[:, 128 * i : 128 * (i + 1)] for i in range(tiles)]
    pieces += [last]
    first = lax.broadcasted_iota(jnp.int32, (8, 128), 0) < vectors
    for fr in range(parts):
        base = fr // 2 * 8
        same = [piece[base : base + 8] for piece in pieces]
        other = [pltpu.roll(piece, vectors, 0) for piece in same]
        low, high = (same, other) if fr % 2 == 0 else (other, same)
        quarters = 2 * list(range(len(pieces)))
        slab = [jnp.where(first, low[i], high[j]) for i, j in zip(quarters[0::2], quarters[1::2])]
        slab = jnp.concatenate(slab, axis=0).astype(BF16)
        for pair in range(columns // 2):
            send_ref[fr * columns // 2 + pair] = slab


def gram_kernel(columns, tiles_ref, out_ref, gram_ref):
    pairs, depth, _ = tiles_ref.shape
    vectors = 4
    count, tiles = 2 * pairs, depth // (2 * vectors)
    wide = count // columns
    half_z = columns // 2
    half_first = FIRST_Z // 2
    places = [
        (x - FIRST_X) % wide * half_z + (z - half_first) % half_z for x in range(wide) for z in range(half_z)
    ]
    slabs = jnp.stack([tiles_ref[n] for n in places]).astype(F32)
    eights = [slabs[:, 8 * k : 8 * (k + 1)] for k in range(tiles)]
    first = lax.broadcasted_iota(jnp.int32, (pairs, 8, 128), 1) < vectors
    half = tiles // 2
    columns_of = []
    for i in range(tiles):
        if i % 2 == 0:
            both = jnp.where(first, eights[i // 2], eights[half + i // 2])
        else:
            both = jnp.where(first, eights[half + (i + 1) // 2], eights[i // 2])
            both = pltpu.roll(both, vectors, 1)
        columns_of.append(both.reshape(count * vectors, 128).astype(BF16))
    both = jnp.concatenate(columns_of, axis=1)
    gram = lax.dot_general(both, both, NT, preferred_element_type=F32)
    gram_ref[...] = gram.reshape(gram_ref.shape)
    z = lax.axis_index("z")
    rows = [gram_ref[(x + FIRST_X) % wide, lax.div(z, 2)] for x in range(wide)]
    rows = [jnp.where(lax.rem(z, 2) == 0, row, pltpu.roll(row, vectors, 0)) for row in rows]
    first = lax.broadcasted_iota(jnp.int32, (8, 128), 0) < vectors
    rows = [jnp.where(first, rows[x], pltpu.roll(rows[x + 1], vectors, 0)) for x in range(0, wide, 2)]
    block = jnp.concatenate(rows, axis=0).astype(BF16)
    for b in range(out_ref.shape[0]):
        out_ref[b] = block


def finish_kernel(scale, parts_ref, even_in_ref, odd_in_ref, inner_ref, even_ref, odd_ref):
    _, vectors, fields, parts, _ = even_ref.shape
    for f in range(fields):
        for r in range(parts):
            for v in range(vectors):
                row = (f * parts + r) * vectors + v
                even_ref[0, v, f, r : r + 1, :] = even_in_ref[row : row + 1]
                odd_ref[0, v, f, r : r + 1, :] = odd_in_ref[row : row + 1]
    total = jnp.sum(parts_ref[...].astype(F32), axis=0)
    inner_ref[...] = (total[:vectors] + total[vectors:]) * scale


VMEM = pl.BlockSpec(memory_space=pltpu.VMEM)
HBM = pl.BlockSpec(memory_space=pltpu.HBM)
PARAMS = pltpu.CompilerParams(vmem_limit_bytes=32 * 1024 * 1024)


def in_hbm(array):
    return pltpu.with_memory_space_constraint(array, pltpu.HBM)


def fourier(wlist, trunc, grid):
    vectors, fields, lats, lons = grid.shape
    bands = wlist.shape[0]
    depth = 4 * vectors * fields
    return pl.pallas_call(
        fourier_kernel,
        name="fourier",
        out_shape=(
            jax.ShapeDtypeStruct((bands, depth, 128), BF16),
            jax.ShapeDtypeStruct((8, 128), jnp.int32),
        ),
        in_specs=[HBM, HBM, HBM],
        out_specs=(VMEM, VMEM),
        scratch_shapes=[
            pltpu.SMEM((bands,), jnp.int32),
            pltpu.VMEM((1, lats), jnp.int32),
            pltpu.VMEM(grid.shape, BF16),
            pltpu.VMEM((4 * bands, lons), BF16),
            pltpu.VMEM((bands * depth, 128), F32),
            pltpu.SemaphoreType.DMA((2,)),
            pltpu.SemaphoreType.DMA((2,)),
        ],
        compiler_params=PARAMS,
    )(in_hbm(wlist), in_hbm(trunc.reshape(1, lats)), in_hbm(grid))


def legendre(own, received, leg_even, leg_odd, vectors, tans):
    depth = received.shape[1]
    hemisphere = leg_odd.shape[2]
    return pl.pallas_call(
        legendre_kernel,
        name="legendre",
        out_shape=(
            jax.ShapeDtypeStruct((tans // 2, 2 * (hemisphere // 64 + 1) * vectors, 128), BF16),
            jax.ShapeDtypeStruct((depth // 2, leg_even.shape[2]), F32),
            jax.ShapeDtypeStruct((depth // 2, leg_odd.shape[2]), F32),
        ),
        in_specs=[VMEM] * 4,
        out_specs=(VMEM, VMEM, VMEM),
        scratch_shapes=[pltpu.VMEM((2, depth, hemisphere), F32)],
        compiler_params=PARAMS,
    )(own, received, jnp.swapaxes(leg_even, 1, 2), leg_odd)


def gram(tiles, columns, bands, vectors):
    tans = 2 * tiles.shape[0]
    wide = tans // columns
    return pl.pallas_call(
        functools.partial(gram_kernel, columns),
        name="gram",
        out_shape=jax.ShapeDtypeStruct((bands, wide * vectors, vectors * tans), BF16),
        in_specs=[VMEM],
        out_specs=VMEM,
        scratch_shapes=[pltpu.VMEM((wide, columns // 2, 2 * vectors, vectors * tans), F32)],
        compiler_params=PARAMS,
    )(tiles)


def finish(products, even, odd, scale, vectors, fields):
    return pl.pallas_call(
        functools.partial(finish_kernel, scale),
        name="finish",
        out_shape=(
            jax.ShapeDtypeStruct((vectors, products.shape[2]), F32),
            jax.ShapeDtypeStruct((1, vectors, fields, 2, even.shape[1]), F32),
            jax.ShapeDtypeStruct((1, vectors, fields, 2, odd.shape[1]), F32),
        ),
        in_specs=[VMEM] * 3,
        out_specs=(VMEM, VMEM, VMEM),
        compiler_params=PARAMS,
    )(products, even, odd)


def on_device(grid, trunc, wlist, leg_even, leg_odd):
    bands = lax.axis_size("band")
    columns = lax.axis_size("z")
    tans = lax.axis_size(("x", "z"))
    vectors, fields, lats, _ = grid.shape
    total_lat = lats * bands
    lat_rows, own = fourier(wlist, trunc, grid)
    received = lax.all_to_all(
        lat_rows, "band", 0, 0, axis_index_groups=[turned(bands, FIRST_BAND)], tiled=True
    )
    tiles, even, odd = legendre(own, received, leg_even, leg_odd, vectors, tans)
    slab = tiles.shape
    tiles = tiles.reshape(tans, slab[1] // (2 * vectors), vectors, 128)
    wide = tans // columns
    tan_group = [x * columns + z for x in turned(wide, FIRST_X) for z in turned(columns, FIRST_Z)]
    tiles = lax.all_to_all(tiles, ("x", "z"), 0, 0, axis_index_groups=[tan_group], tiled=True)
    products = gram(tiles.reshape(slab), columns, bands, vectors)
    products = products.reshape(-1, vectors, vectors * tans)
    group = [b * wide + x for b in turned(bands, FIRST_BAND) for x in turned(wide, FIRST_X)]
    products = lax.all_to_all(products, ("band", "x"), 0, 0, axis_index_groups=[group], tiled=True)
    products = products.reshape(-1, 2 * vectors, vectors * tans)
    scale = 1.0 / (bands * 4.0 * (total_lat + 1))
    inner, even, odd = finish(products, even, odd, scale, vectors, fields)
    return (even, odd, inner.T)


def solution(mesh):
    bands, tans = mesh.devices.shape
    split = jax.sharding.Mesh(mesh.devices.reshape(bands, 4, tans // 4), ("band", "x", "z"))
    tan = ("x", "z")
    return jax.shard_map(
        on_device,
        mesh=split,
        in_specs=(
            P(tan, None, "band", None),
            P("band"),
            P(),
            P("band", None, None),
            P("band", None, None),
        ),
        out_specs=(
            P("band", tan, None, None, None),
            P("band", tan, None, None, None),
            P(None, tan),
        ),
        check_vma=False,
    )
```

```python
import functools
import math

import jax
import jax.numpy as jnp
from jax import lax
from jax.experimental import pallas as pl
from jax.experimental.pallas import tpu as pltpu
from jax.sharding import PartitionSpec as P

F32 = jnp.float32
FOURIER_BANDS = [11, 12, 13, 14, 15, 0, 1, 2, 3, 4, 5, 6, 7, 8, 9, 10]
TILE_PAIRS = [
    (2, 3), (1, 3), (3, 3), (0, 3), (2, 0), (2, 2), (1, 0), (1, 2),
    (3, 0), (3, 2), (0, 0), (0, 2), (2, 1), (1, 1), (3, 1), (0, 1),
]
PRODUCT_BANDS = [11, 2, 3, 0, 4, 1, 5, 6, 14, 7, 15, 8, 12, 9, 13, 10]
PRODUCT_XS = [2, 0, 1, 3]
BF16 = jnp.bfloat16
NT = (((1,), (1,)), ((), ()))
NN = (((1,), (0,)), ((), ()))


def table_kernel(lats, lons, wlist_hbm, trunc_hbm, table, keep_ref, own_ref, wlist_ref, trunc_ref, small):
    bands = wlist_ref.shape[0]
    total_lat = lats * bands
    members = 2 * bands
    get_wlist = pltpu.make_async_copy(wlist_hbm, wlist_ref, small.at[0])
    get_trunc = pltpu.make_async_copy(trunc_hbm, trunc_ref, small.at[1])
    get_wlist.start()
    get_trunc.start()
    row = lax.broadcasted_iota(jnp.int32, (members, 128), 0)
    lane = lax.broadcasted_iota(jnp.int32, (members, 128), 1)
    get_wlist.wait()
    mvals = jnp.zeros((members, 128), jnp.int32)
    for b in range(bands):
        wave, place = wlist_ref[b], FOURIER_BANDS.index(b)
        mvals = jnp.where(row == place, wave, mvals)
        mvals = jnp.where(row == bands + place, total_lat - 1 - wave, mvals)
    own_ref[...] = jnp.full(own_ref.shape, wlist_ref[lax.axis_index("band")], jnp.int32)
    unit = 2.0 * math.pi / lons
    scaling = 1.0 / math.sqrt(lons)
    chunks = lons // 128
    fine = (mvals * lane % lons).astype(F32) * unit
    coarse = (mvals * lane % chunks).astype(F32) * (128.0 * unit)
    fine_cos, fine_sin = jnp.cos(fine), jnp.sin(fine)
    coarse_cos, coarse_sin = jnp.cos(coarse) * scaling, jnp.sin(coarse) * scaling
    for i in range(chunks):
        cc, cs = coarse_cos[:, i : i + 1], coarse_sin[:, i : i + 1]
        table[:members, 128 * i : 128 * (i + 1)] = (cc * fine_cos - cs * fine_sin).astype(BF16)
        table[members:, 128 * i : 128 * (i + 1)] = (-(cs * fine_cos + cc * fine_sin)).astype(BF16)
    get_trunc.wait()
    keep = mvals[:, :lats] <= trunc_ref[...]
    keep = jnp.where(keep, 1.0, 0.0)
    keep_ref[...] = jnp.concatenate([keep, keep], axis=0)


def pack_kernel(spectra_ref, keep_ref, out_ref, rows):
    bands = out_ref.shape[0]
    lats = keep_ref.shape[1]
    fields, vectors = 2, spectra_ref.shape[1] // (2 * lats)
    keep = keep_ref[...] > 0
    depth = out_ref.shape[1]
    wide = lax.broadcasted_iota(jnp.int32, (bands, 128), 1)
    for v in range(vectors):
        fields_of = []
        for f in range(fields):
            place = lats * (v * fields + f)
            spectra = spectra_ref[:, place : place + lats]
            spectra = jnp.where(keep, spectra, 0.0)
            fields_of.append(jnp.pad(spectra, ((0, 0), (0, 128 - lats))))
        for r in range(2):
            others = jnp.zeros((bands, 128), F32)
            for p in range(2):
                start = (r * 2 + p) * bands
                one, two = (spectra[start : start + bands] for spectra in fields_of)
                rows[pl.ds((p * 2 + r) * vectors + v, bands, stride=depth), :] = jnp.where(
                    wide < 64, one, pltpu.roll(two, 64, 1)
                )
                for f, spectra in enumerate((one, two)):
                    place = 16 * (p * fields + f)
                    mine = (wide >= place) & (wide < place + 16)
                    others = jnp.where(mine, pltpu.roll(spectra, (place + 64) % 128, 1), others)
            rows[pl.ds((4 + r) * vectors + v, bands, stride=depth), :] = others
    out_ref[...] = rows[...].astype(BF16).reshape(out_ref.shape)


def legendre_kernel(own_ref, rows_ref, even_t_ref, odd_ref, send_ref, even_ref, odd_out_ref, fold):
    bands = rows_ref.shape[0]
    half_bands = bands // 2
    hemisphere = odd_ref.shape[1]
    lats = hemisphere // half_bands
    total_lat = 2 * hemisphere
    depth = fold.shape[1]
    own = own_ref[0:1, 0:1]

    def slab(band):
        packed = rows_ref[FOURIER_BANDS.index(band)].astype(F32)
        others = packed[2 * depth // 4 :]
        groups = []
        for p in range(2):
            for f in range(2):
                main = packed[p * depth // 4 : (p + 1) * depth // 4]
                main = pltpu.roll(main, 64, 1) if f else main
                groups.append(jnp.where(low, main, pltpu.roll(others, 64 - 16 * (p * 2 + f), 1)))
        return jnp.concatenate(groups, axis=0)

    ri = lax.broadcasted_iota(jnp.int32, (128, 128), 0)
    ci = lax.broadcasted_iota(jnp.int32, (128, 128), 1)
    low = ci[: depth // 4] < 64
    mirror = jnp.where(ri + ci == lats - 1, 1.0, 0.0).astype(BF16)
    south = jnp.concatenate([slab(b) for b in range(half_bands, bands)], axis=0).astype(BF16)
    south = lax.dot_general(south, mirror, NN, preferred_element_type=F32)
    for b in range(half_bands):
        north_b = slab(b)
        s = half_bands - 1 - b
        south_b = south[s * depth : (s + 1) * depth]
        fold[0, :, lats * b : lats * (b + 1)] = (north_b + south_b)[:, :lats]
        fold[1, :, lats * b : lats * (b + 1)] = (north_b - south_b)[:, :lats]
    sym, anti = fold[0].astype(BF16), fold[1].astype(BF16)
    even_all = lax.dot_general(sym, even_t_ref[0], NT, preferred_element_type=F32)
    odd_all = lax.dot_general(anti, odd_ref[0], NN, preferred_element_type=F32)
    half = depth // 2
    even_col = lax.broadcasted_iota(jnp.int32, (half, hemisphere + 1), 1)
    odd_col = lax.broadcasted_iota(jnp.int32, (half, hemisphere), 1)
    even = jnp.where(even_col < ((total_lat + 1 - own) >> 1), even_all[:half], even_all[half:])
    odd = jnp.where(odd_col < ((total_lat - own) >> 1), odd_all[:half], odd_all[half:])
    even_ref[...] = even
    odd_out_ref[...] = odd
    tiles = hemisphere // 128
    vectors = 4
    parts = half // vectors
    columns = 2 * send_ref.shape[0] // parts
    last = jnp.broadcast_to(even[:, hemisphere : hemisphere + 1], (half, 128))
    last = jnp.where(lax.broadcasted_iota(jnp.int32, (half, 128), 1) == 0, last, 0.0)
    pieces = [even[:, 128 * i : 128 * (i + 1)] for i in range(tiles)]
    pieces += [odd[:, 128 * i : 128 * (i + 1)] for i in range(tiles)]
    pieces += [last]
    first = lax.broadcasted_iota(jnp.int32, (8, 128), 0) < vectors
    for fr in range(parts):
        base = fr // 2 * 8
        same = [piece[base : base + 8] for piece in pieces]
        other = [pltpu.roll(piece, vectors, 0) for piece in same]
        low, high = (same, other) if fr % 2 == 0 else (other, same)
        quarters = 2 * list(range(len(pieces)))
        slab = [jnp.where(first, low[i], high[j]) for i, j in zip(quarters[0::2], quarters[1::2])]
        slab = jnp.concatenate(slab, axis=0).astype(BF16)
        for place, (x, _) in enumerate(TILE_PAIRS):
            if x == fr:
                send_ref[place] = slab


def gram_kernel(columns, tiles_ref, out_ref, gram_ref):
    pairs, depth, _ = tiles_ref.shape
    vectors = 4
    count, tiles = 2 * pairs, depth // (2 * vectors)
    wide = count // columns
    half_z = columns // 2
    places = [TILE_PAIRS.index((x, z)) for x in range(wide) for z in range(columns // 2)]
    slabs = jnp.stack([tiles_ref[n] for n in places]).astype(F32)
    eights = [slabs[:, 8 * k : 8 * (k + 1)] for k in range(tiles)]
    first = lax.broadcasted_iota(jnp.int32, (pairs, 8, 128), 1) < vectors
    half = tiles // 2
    columns_of = []
    for i in range(tiles):
        if i % 2 == 0:
            both = jnp.where(first, eights[i // 2], eights[half + i // 2])
        else:
            both = jnp.where(first, eights[half + (i + 1) // 2], eights[i // 2])
            both = pltpu.roll(both, vectors, 1)
        columns_of.append(both.reshape(count * vectors, 128).astype(BF16))
    both = jnp.concatenate(columns_of, axis=1)
    gram = lax.dot_general(both, both, NT, preferred_element_type=F32)
    gram_ref[...] = gram.reshape(gram_ref.shape)
    z = lax.axis_index("z")
    rows = [gram_ref[x, lax.div(z, 2)] for x in PRODUCT_XS]
    rows = [jnp.where(lax.rem(z, 2) == 0, row, pltpu.roll(row, vectors, 0)) for row in rows]
    first = lax.broadcasted_iota(jnp.int32, (8, 128), 0) < vectors
    rows = [jnp.where(first, rows[x], pltpu.roll(rows[x + 1], vectors, 0)) for x in range(0, wide, 2)]
    block = jnp.concatenate(rows, axis=0).astype(BF16)
    for b in range(out_ref.shape[0]):
        out_ref[b] = block


def finish_kernel(scale, parts_ref, even_in_ref, odd_in_ref, inner_ref, even_ref, odd_ref):
    _, vectors, fields, parts, _ = even_ref.shape
    for f in range(fields):
        for r in range(parts):
            for v in range(vectors):
                row = (f * parts + r) * vectors + v
                even_ref[0, v, f, r : r + 1, :] = even_in_ref[row : row + 1]
                odd_ref[0, v, f, r : r + 1, :] = odd_in_ref[row : row + 1]
    total = jnp.sum(parts_ref[...].astype(F32), axis=0)
    inner_ref[...] = (total[:vectors] + total[vectors:]) * scale


VMEM = pl.BlockSpec(memory_space=pltpu.VMEM)
HBM = pl.BlockSpec(memory_space=pltpu.HBM)
PARAMS = pltpu.CompilerParams(vmem_limit_bytes=32 * 1024 * 1024)


def in_hbm(array):
    return pltpu.with_memory_space_constraint(array, pltpu.HBM)


def fourier(wlist, trunc, grid):
    vectors, fields, lats, lons = grid.shape
    bands = wlist.shape[0]
    depth = 6 * vectors
    table, keep, own = pl.pallas_call(
        functools.partial(table_kernel, lats, lons),
        name="table",
        out_shape=(
            jax.ShapeDtypeStruct((4 * bands, lons), BF16),
            jax.ShapeDtypeStruct((4 * bands, lats), F32),
            jax.ShapeDtypeStruct((8, 128), jnp.int32),
        ),
        in_specs=[HBM, HBM],
        out_specs=(VMEM, VMEM, VMEM),
        scratch_shapes=[
            pltpu.SMEM((bands,), jnp.int32),
            pltpu.VMEM((1, lats), jnp.int32),
            pltpu.SemaphoreType.DMA((2,)),
        ],
        compiler_params=PARAMS,
    )(in_hbm(wlist), in_hbm(trunc.reshape(1, lats)))
    spectra = lax.dot_general(table, grid.reshape(-1, lons), NT, preferred_element_type=F32)
    lat_rows = pl.pallas_call(
        pack_kernel,
        name="pack",
        out_shape=jax.ShapeDtypeStruct((bands, depth, 128), BF16),
        in_specs=[VMEM, VMEM],
        out_specs=VMEM,
        scratch_shapes=[pltpu.VMEM((bands * depth, 128), F32)],
        compiler_params=PARAMS,
    )(spectra, keep)
    return lat_rows, own


def legendre(own, received, leg_even, leg_odd, vectors, tans):
    depth = 8 * vectors
    hemisphere = leg_odd.shape[2]
    return pl.pallas_call(
        legendre_kernel,
        name="legendre",
        out_shape=(
            jax.ShapeDtypeStruct((tans // 2, 2 * (hemisphere // 64 + 1) * vectors, 128), BF16),
            jax.ShapeDtypeStruct((depth // 2, leg_even.shape[2]), F32),
            jax.ShapeDtypeStruct((depth // 2, leg_odd.shape[2]), F32),
        ),
        in_specs=[VMEM] * 4,
        out_specs=(VMEM, VMEM, VMEM),
        scratch_shapes=[pltpu.VMEM((2, depth, hemisphere), F32)],
        compiler_params=PARAMS,
    )(own, received, jnp.swapaxes(leg_even, 1, 2), leg_odd)


def gram(tiles, columns, bands, vectors):
    tans = 2 * tiles.shape[0]
    wide = tans // columns
    return pl.pallas_call(
        functools.partial(gram_kernel, columns),
        name="gram",
        out_shape=jax.ShapeDtypeStruct((bands, wide * vectors, vectors * tans), BF16),
        in_specs=[VMEM],
        out_specs=VMEM,
        scratch_shapes=[pltpu.VMEM((wide, columns // 2, 2 * vectors, vectors * tans), F32)],
        compiler_params=PARAMS,
    )(tiles)


def finish(products, even, odd, scale, vectors, fields):
    return pl.pallas_call(
        functools.partial(finish_kernel, scale),
        name="finish",
        out_shape=(
            jax.ShapeDtypeStruct((vectors, products.shape[2]), F32),
            jax.ShapeDtypeStruct((1, vectors, fields, 2, even.shape[1]), F32),
            jax.ShapeDtypeStruct((1, vectors, fields, 2, odd.shape[1]), F32),
        ),
        in_specs=[VMEM] * 3,
        out_specs=(VMEM, VMEM, VMEM),
        compiler_params=PARAMS,
    )(products, even, odd)


def on_device(grid, trunc, wlist, leg_even, leg_odd):
    bands = lax.axis_size("band")
    columns = lax.axis_size("z")
    tans = lax.axis_size(("x", "z"))
    vectors, fields, lats, _ = grid.shape
    total_lat = lats * bands
    lat_rows, own = fourier(wlist, trunc, grid)
    received = lax.all_to_all(
        lat_rows, "band", 0, 0, axis_index_groups=[FOURIER_BANDS], tiled=True
    )
    tiles, even, odd = legendre(own, received, leg_even, leg_odd, vectors, tans)
    slab = tiles.shape
    tiles = tiles.reshape(tans, slab[1] // (2 * vectors), vectors, 128)
    wide = tans // columns
    tan_group = [x * columns + 2 * z + n for x, z in TILE_PAIRS for n in range(2)]
    tiles = lax.all_to_all(tiles, ("x", "z"), 0, 0, axis_index_groups=[tan_group], tiled=True)
    products = gram(tiles.reshape(slab), columns, bands, vectors)
    products = products.reshape(-1, vectors, vectors * tans)
    group = [b * wide + x for b in PRODUCT_BANDS for x in PRODUCT_XS]
    products = lax.all_to_all(products, ("band", "x"), 0, 0, axis_index_groups=[group], tiled=True)
    products = products.reshape(-1, 2 * vectors, vectors * tans)
    scale = 1.0 / (bands * 4.0 * (total_lat + 1))
    inner, even, odd = finish(products, even, odd, scale, vectors, fields)
    return (even, odd, inner.T)


def solution(mesh):
    bands, tans = mesh.devices.shape
    split = jax.sharding.Mesh(mesh.devices.reshape(bands, 4, tans // 4), ("band", "x", "z"))
    tan = ("x", "z")
    return jax.shard_map(
        on_device,
        mesh=split,
        in_specs=(
            P(tan, None, "band", None),
            P("band"),
            P(),
            P("band", None, None),
            P("band", None, None),
        ),
        out_specs=(
            P("band", tan, None, None, None),
            P("band", tan, None, None, None),
            P(None, tan),
        ),
        check_vma=False,
    )
```

```python
import functools
import math

import jax
import jax.numpy as jnp
from jax import lax
from jax.experimental import pallas as pl
from jax.experimental.pallas import tpu as pltpu
from jax.sharding import PartitionSpec as P

F32 = jnp.float32
FOURIER_BANDS = [11, 12, 13, 14, 15, 0, 1, 2, 3, 4, 5, 6, 7, 8, 9, 10]
TILE_PAIRS = [
    (2, 3), (1, 3), (3, 3), (0, 3), (2, 0), (2, 2), (1, 0), (1, 2),
    (3, 0), (3, 2), (0, 0), (0, 2), (2, 1), (1, 1), (3, 1), (0, 1),
]
PRODUCT_BANDS = [11, 2, 3, 0, 4, 1, 5, 6, 14, 7, 15, 8, 12, 9, 13, 10]
PRODUCT_XS = [2, 0, 1, 3]
BF16 = jnp.bfloat16
NT = (((1,), (1,)), ((), ()))
NN = (((1,), (0,)), ((), ()))


def table_kernel(lats, lons, wlist_hbm, trunc_hbm, table, keep_ref, own_ref, wlist_ref, trunc_ref, small):
    bands = wlist_ref.shape[0]
    total_lat = lats * bands
    members = 2 * bands
    get_wlist = pltpu.make_async_copy(wlist_hbm, wlist_ref, small.at[0])
    get_trunc = pltpu.make_async_copy(trunc_hbm, trunc_ref, small.at[1])
    get_wlist.start()
    get_trunc.start()
    row = lax.broadcasted_iota(jnp.int32, (members, 128), 0)
    lane = lax.broadcasted_iota(jnp.int32, (members, 128), 1)
    get_wlist.wait()
    mvals = jnp.zeros((members, 128), jnp.int32)
    for b in range(bands):
        wave, place = wlist_ref[b], FOURIER_BANDS.index(b)
        mvals = jnp.where(row == place, wave, mvals)
        mvals = jnp.where(row == bands + place, total_lat - 1 - wave, mvals)
    own_ref[...] = jnp.full(own_ref.shape, wlist_ref[lax.axis_index("band")], jnp.int32)
    unit = 2.0 * math.pi / lons
    scaling = 1.0 / math.sqrt(lons)
    chunks = lons // 128
    fine = (mvals * lane % lons).astype(F32) * unit
    coarse = (mvals * lane % chunks).astype(F32) * (128.0 * unit)
    fine_cos, fine_sin = jnp.cos(fine), jnp.sin(fine)
    coarse_cos, coarse_sin = jnp.cos(coarse) * scaling, jnp.sin(coarse) * scaling
    for i in range(chunks):
        cc, cs = coarse_cos[:, i : i + 1], coarse_sin[:, i : i + 1]
        table[:members, 128 * i : 128 * (i + 1)] = (cc * fine_cos - cs * fine_sin).astype(BF16)
        table[members:, 128 * i : 128 * (i + 1)] = (-(cs * fine_cos + cc * fine_sin)).astype(BF16)
    get_trunc.wait()
    keep = mvals[:, :lats] <= trunc_ref[...]
    keep = jnp.where(keep, 1.0, 0.0)
    keep_ref[...] = jnp.concatenate([keep, keep], axis=0)


def pack_kernel(spectra_ref, keep_ref, out_ref, rows):
    bands = out_ref.shape[0]
    lats = keep_ref.shape[1]
    fields, vectors = 2, spectra_ref.shape[1] // (2 * lats)
    keep = keep_ref[...] > 0
    depth = out_ref.shape[1]
    wide = lax.broadcasted_iota(jnp.int32, (bands, 128), 1)
    for v in range(vectors):
        fields_of = []
        for f in range(fields):
            place = lats * (v * fields + f)
            spectra = spectra_ref[:, place : place + lats]
            spectra = jnp.where(keep, spectra, 0.0)
            fields_of.append(jnp.pad(spectra, ((0, 0), (0, 128 - lats))))
        for r in range(2):
            others = jnp.zeros((bands, 128), F32)
            for p in range(2):
                start = (r * 2 + p) * bands
                one, two = (spectra[start : start + bands] for spectra in fields_of)
                rows[pl.ds((p * 2 + r) * vectors + v, bands, stride=depth), :] = jnp.where(
                    wide < 64, one, pltpu.roll(two, 64, 1)
                )
                for f, spectra in enumerate((one, two)):
                    place = 16 * (p * fields + f)
                    mine = (wide >= place) & (wide < place + 16)
                    others = jnp.where(mine, pltpu.roll(spectra, (place + 64) % 128, 1), others)
            rows[pl.ds((4 + r) * vectors + v, bands, stride=depth), :] = others
    out_ref[...] = rows[...].astype(BF16).reshape(out_ref.shape)


def legendre_kernel(own_ref, rows_ref, even_t_ref, odd_ref, send_ref, even_ref, odd_out_ref, fold):
    bands = rows_ref.shape[0]
    half_bands = bands // 2
    hemisphere = odd_ref.shape[1]
    lats = hemisphere // half_bands
    total_lat = 2 * hemisphere
    depth = fold.shape[1]
    own = own_ref[0:1, 0:1]

    def slab(band):
        packed = rows_ref[FOURIER_BANDS.index(band)].astype(F32)
        others = packed[2 * depth // 4 :]
        groups = []
        for p in range(2):
            for f in range(2):
                main = packed[p * depth // 4 : (p + 1) * depth // 4]
                main = pltpu.roll(main, 64, 1) if f else main
                groups.append(jnp.where(low, main, pltpu.roll(others, 64 - 16 * (p * 2 + f), 1)))
        return jnp.concatenate(groups, axis=0)

    ri = lax.broadcasted_iota(jnp.int32, (128, 128), 0)
    ci = lax.broadcasted_iota(jnp.int32, (128, 128), 1)
    low = ci[: depth // 4] < 64
    mirror = jnp.where(ri + ci == lats - 1, 1.0, 0.0).astype(BF16)
    south = jnp.concatenate([slab(b) for b in range(half_bands, bands)], axis=0).astype(BF16)
    south = lax.dot_general(south, mirror, NN, preferred_element_type=F32)
    for b in range(half_bands):
        north_b = slab(b)
        s = half_bands - 1 - b
        south_b = south[s * depth : (s + 1) * depth]
        fold[0, :, lats * b : lats * (b + 1)] = (north_b + south_b)[:, :lats]
        fold[1, :, lats * b : lats * (b + 1)] = (north_b - south_b)[:, :lats]
    sym, anti = fold[0].astype(BF16), fold[1].astype(BF16)
    even_all = lax.dot_general(sym, even_t_ref[0], NT, preferred_element_type=F32)
    odd_all = lax.dot_general(anti, odd_ref[0], NN, preferred_element_type=F32)
    half = depth // 2
    even_col = lax.broadcasted_iota(jnp.int32, (half, hemisphere + 1), 1)
    odd_col = lax.broadcasted_iota(jnp.int32, (half, hemisphere), 1)
    even = jnp.where(even_col < ((total_lat + 1 - own) >> 1), even_all[:half], even_all[half:])
    odd = jnp.where(odd_col < ((total_lat - own) >> 1), odd_all[:half], odd_all[half:])
    even_ref[...] = even
    odd_out_ref[...] = odd
    tiles = hemisphere // 128
    vectors = 4
    parts = half // vectors
    columns = 2 * send_ref.shape[0] // parts
    last = jnp.broadcast_to(even[:, hemisphere : hemisphere + 1], (half, 128))
    last = jnp.where(lax.broadcasted_iota(jnp.int32, (half, 128), 1) == 0, last, 0.0)
    pieces = [even[:, 128 * i : 128 * (i + 1)] for i in range(tiles)] + [last]
    pieces += [odd[:, 128 * i : 128 * (i + 1)] for i in range(tiles)] + [jnp.zeros_like(last)]
    first = lax.broadcasted_iota(jnp.int32, (8, 128), 0) < vectors
    for fr in range(parts):
        base = fr // 2 * 8
        same = [piece[base : base + 8] for piece in pieces]
        other = [pltpu.roll(piece, vectors, 0) for piece in same]
        low, high = (same, other) if fr % 2 == 0 else (other, same)
        eights = [jnp.where(first, low[i], high[i + 1]) for i in range(0, len(pieces), 2)]
        block = jnp.concatenate(eights, axis=0).astype(BF16)
        for place, (x, _) in enumerate(TILE_PAIRS):
            if x == fr:
                send_ref[place] = block


def gram_kernel(columns, tiles_ref, out_ref, gram_ref):
    pairs, depth, _ = tiles_ref.shape
    wide = pairs // (columns // 2)
    places = [TILE_PAIRS.index((x, z)) for x in range(wide) for z in range(columns // 2)]
    slabs = jnp.stack([tiles_ref[n] for n in places]).astype(F32)
    eights = [slabs[:, 8 * k : 8 * (k + 1)] for k in range(depth // 8)]
    half = len(eights) // 2
    first = lax.broadcasted_iota(jnp.int32, (pairs, 8, 128), 1) < 4
    quarters = []
    for one, two in zip(eights[:half], eights[half:]):
        quarters.append(jnp.where(first, one, pltpu.roll(two, 4, 1)))
        quarters.append(jnp.where(first, pltpu.roll(one, 4, 1), two))
    both = [quarter.reshape(8 * pairs, 128).astype(BF16) for quarter in quarters]
    both = jnp.concatenate(both, axis=1)
    gram = lax.dot_general(both, both, NT, preferred_element_type=F32)
    gram_ref[...] = gram.reshape(gram_ref.shape)
    own = lax.div(lax.axis_index("z"), 2)
    blocks = [gram_ref[x, own].astype(BF16) for x in PRODUCT_XS]
    for n in range(out_ref.shape[0]):
        out_ref[n] = blocks[n % wide]


def finish_kernel(scale, parts_ref, even_in_ref, odd_in_ref, inner_ref, even_ref, odd_ref):
    _, vectors, fields, parts, _ = even_ref.shape
    for f in range(fields):
        for r in range(parts):
            for v in range(vectors):
                row = (f * parts + r) * vectors + v
                even_ref[0, v, f, r : r + 1, :] = even_in_ref[row : row + 1]
                odd_ref[0, v, f, r : r + 1, :] = odd_in_ref[row : row + 1]
    total = jnp.sum(parts_ref[...].astype(F32), axis=0)
    inner_ref[...] = (total[:vectors] + total[vectors:]) * scale


VMEM = pl.BlockSpec(memory_space=pltpu.VMEM)
HBM = pl.BlockSpec(memory_space=pltpu.HBM)
PARAMS = pltpu.CompilerParams(vmem_limit_bytes=32 * 1024 * 1024)


def in_hbm(array):
    return pltpu.with_memory_space_constraint(array, pltpu.HBM)


def fourier(wlist, trunc, grid):
    vectors, fields, lats, lons = grid.shape
    bands = wlist.shape[0]
    depth = 6 * vectors
    table, keep, own = pl.pallas_call(
        functools.partial(table_kernel, lats, lons),
        name="table",
        out_shape=(
            jax.ShapeDtypeStruct((4 * bands, lons), BF16),
            jax.ShapeDtypeStruct((4 * bands, lats), F32),
            jax.ShapeDtypeStruct((8, 128), jnp.int32),
        ),
        in_specs=[HBM, HBM],
        out_specs=(VMEM, VMEM, VMEM),
        scratch_shapes=[
            pltpu.SMEM((bands,), jnp.int32),
            pltpu.VMEM((1, lats), jnp.int32),
            pltpu.SemaphoreType.DMA((2,)),
        ],
        compiler_params=PARAMS,
    )(in_hbm(wlist), in_hbm(trunc.reshape(1, lats)))
    spectra = lax.dot_general(table, grid.reshape(-1, lons), NT, preferred_element_type=F32)
    lat_rows = pl.pallas_call(
        pack_kernel,
        name="pack",
        out_shape=jax.ShapeDtypeStruct((bands, depth, 128), BF16),
        in_specs=[VMEM, VMEM],
        out_specs=VMEM,
        scratch_shapes=[pltpu.VMEM((bands * depth, 128), F32)],
        compiler_params=PARAMS,
    )(spectra, keep)
    return lat_rows, own


def legendre(own, received, leg_even, leg_odd, vectors, tans):
    depth = 8 * vectors
    hemisphere = leg_odd.shape[2]
    return pl.pallas_call(
        legendre_kernel,
        name="legendre",
        out_shape=(
            jax.ShapeDtypeStruct((tans // 2, 2 * (hemisphere // 128 + 1) * vectors, 128), BF16),
            jax.ShapeDtypeStruct((depth // 2, leg_even.shape[2]), F32),
            jax.ShapeDtypeStruct((depth // 2, leg_odd.shape[2]), F32),
        ),
        in_specs=[VMEM] * 4,
        out_specs=(VMEM, VMEM, VMEM),
        scratch_shapes=[pltpu.VMEM((2, depth, hemisphere), F32)],
        compiler_params=PARAMS,
    )(own, received, jnp.swapaxes(leg_even, 1, 2), leg_odd)


def gram(tiles, columns, bands, vectors):
    tans = 2 * tiles.shape[0]
    wide = tans // columns
    return pl.pallas_call(
        functools.partial(gram_kernel, columns),
        name="gram",
        out_shape=jax.ShapeDtypeStruct((bands * wide, 2 * vectors, vectors * tans), BF16),
        in_specs=[VMEM],
        out_specs=VMEM,
        scratch_shapes=[pltpu.VMEM((wide, columns // 2, 2 * vectors, vectors * tans), F32)],
        compiler_params=PARAMS,
    )(tiles)


def finish(products, even, odd, scale, vectors, fields):
    return pl.pallas_call(
        functools.partial(finish_kernel, scale),
        name="finish",
        out_shape=(
            jax.ShapeDtypeStruct((vectors, products.shape[2]), F32),
            jax.ShapeDtypeStruct((1, vectors, fields, 2, even.shape[1]), F32),
            jax.ShapeDtypeStruct((1, vectors, fields, 2, odd.shape[1]), F32),
        ),
        in_specs=[VMEM] * 3,
        out_specs=(VMEM, VMEM, VMEM),
        compiler_params=PARAMS,
    )(products, even, odd)


def on_device(grid, trunc, wlist, leg_even, leg_odd):
    bands = lax.axis_size("band")
    columns = lax.axis_size("z")
    tans = lax.axis_size(("x", "z"))
    vectors, fields, lats, _ = grid.shape
    total_lat = lats * bands
    lat_rows, own = fourier(wlist, trunc, grid)
    received = lax.all_to_all(
        lat_rows, "band", 0, 0, axis_index_groups=[FOURIER_BANDS], tiled=True
    )
    tiles, even, odd = legendre(own, received, leg_even, leg_odd, vectors, tans)
    slab = tiles.shape
    tiles = tiles.reshape(tans, slab[1] // 4, 2, 128)
    wide = tans // columns
    tan_group = [x * columns + 2 * z + n for x, z in TILE_PAIRS for n in range(2)]
    tiles = lax.all_to_all(tiles, ("x", "z"), 0, 0, axis_index_groups=[tan_group], tiled=True)
    products = gram(tiles.reshape(slab), columns, bands, vectors)
    products = products.reshape(-1, vectors, vectors * tans)
    product_groups = [
        [(b * wide + x) * columns + z + n for b in PRODUCT_BANDS for x in PRODUCT_XS for n in range(2)]
        for z in range(0, columns, 2)
    ]
    products = lax.all_to_all(products, ("band", "x", "z"), 0, 0, axis_index_groups=product_groups, tiled=True)
    products = products.reshape(-1, 2 * vectors, vectors * tans)
    scale = 1.0 / (bands * 4.0 * (total_lat + 1))
    inner, even, odd = finish(products, even, odd, scale, vectors, fields)
    return (even, odd, inner.T)


def solution(mesh):
    bands, tans = mesh.devices.shape
    split = jax.sharding.Mesh(mesh.devices.reshape(bands, 4, tans // 4), ("band", "x", "z"))
    tan = ("x", "z")
    return jax.shard_map(
        on_device,
        mesh=split,
        in_specs=(
            P(tan, None, "band", None),
            P("band"),
            P(),
            P("band", None, None),
            P("band", None, None),
        ),
        out_specs=(
            P("band", tan, None, None, None),
            P("band", tan, None, None, None),
            P(None, tan),
        ),
        check_vma=False,
    )
```

```python
import functools
import math

import jax
import jax.numpy as jnp
from jax import lax
from jax.experimental import pallas as pl
from jax.experimental.pallas import tpu as pltpu
from jax.sharding import PartitionSpec as P

F32 = jnp.float32
FOURIER_BANDS = [11, 12, 13, 14, 15, 0, 1, 2, 3, 4, 5, 6, 7, 8, 9, 10]
TILE_PAIRS = [
    (2, 3), (1, 3), (3, 3), (0, 3), (2, 0), (2, 2), (1, 0), (1, 2),
    (3, 0), (3, 2), (0, 0), (0, 2), (2, 1), (1, 1), (3, 1), (0, 1),
]
PRODUCT_BANDS = [11, 2, 3, 0, 4, 1, 5, 6, 14, 7, 15, 8, 12, 9, 13, 10]
PRODUCT_XS = [2, 0, 1, 3]
BF16 = jnp.bfloat16
NT = (((1,), (1,)), ((), ()))
NN = (((1,), (0,)), ((), ()))


def cos_sin(phase, count):
    phase = phase % count
    quarter = count // 4
    turn = (phase + quarter // 2) // quarter
    angle = (phase - turn * quarter).astype(F32) * (2.0 * math.pi / count)
    square = angle * angle
    cos = 1.0 + square * (-1 / 2 + square * (1 / 24 + square * (-1 / 720 + square * (1 / 40320))))
    sin = angle * (1.0 + square * (-1 / 6 + square * (1 / 120 + square * (-1 / 5040 + square * (1 / 362880)))))
    odd = (turn & 1) == 1
    cos, sin = jnp.where(odd, sin, cos), jnp.where(odd, cos, sin)
    return jnp.where(((turn + 1) & 2) == 2, -cos, cos), jnp.where((turn & 2) == 2, -sin, sin)


def table_kernel(lats, lons, wlist_hbm, trunc_hbm, table, keep_ref, own_ref, wlist_ref, trunc_ref, small):
    bands = wlist_ref.shape[0]
    total_lat = lats * bands
    members = 2 * bands
    get_wlist = pltpu.make_async_copy(wlist_hbm, wlist_ref, small.at[0])
    get_trunc = pltpu.make_async_copy(trunc_hbm, trunc_ref, small.at[1])
    get_wlist.start()
    get_trunc.start()
    row = lax.broadcasted_iota(jnp.int32, (members, 128), 0)
    lane = lax.broadcasted_iota(jnp.int32, (members, 128), 1)
    get_wlist.wait()
    mvals = jnp.zeros((members, 128), jnp.int32)
    for b in range(bands):
        wave, place = wlist_ref[b], FOURIER_BANDS.index(b)
        mvals = jnp.where(row == place, wave, mvals)
        mvals = jnp.where(row == bands + place, total_lat - 1 - wave, mvals)
    own_ref[...] = jnp.full(own_ref.shape, wlist_ref[lax.axis_index("band")], jnp.int32)
    scaling = 1.0 / math.sqrt(lons)
    chunks = lons // 128
    fine_cos, fine_sin = cos_sin(mvals * lane, lons)
    coarse_cos, coarse_sin = cos_sin(mvals * lane, chunks)
    coarse_cos, coarse_sin = coarse_cos * scaling, coarse_sin * scaling
    for i in range(chunks):
        cc, cs = coarse_cos[:, i : i + 1], coarse_sin[:, i : i + 1]
        table[:members, 128 * i : 128 * (i + 1)] = (cc * fine_cos - cs * fine_sin).astype(BF16)
        table[members:, 128 * i : 128 * (i + 1)] = (-(cs * fine_cos + cc * fine_sin)).astype(BF16)
    get_trunc.wait()
    keep = mvals[:, :lats] <= trunc_ref[...]
    keep = jnp.where(keep, 1.0, 0.0)
    keep_ref[...] = jnp.concatenate([keep, keep], axis=0)


def pack_kernel(spectra_ref, keep_ref, out_ref, rows):
    bands = out_ref.shape[0]
    lats = keep_ref.shape[1]
    fields, vectors = 2, spectra_ref.shape[1] // (2 * lats)
    keep = keep_ref[...] > 0
    depth = out_ref.shape[1]
    wide = lax.broadcasted_iota(jnp.int32, (bands, 128), 1)
    for v in range(vectors):
        fields_of = []
        for f in range(fields):
            place = lats * (v * fields + f)
            spectra = spectra_ref[:, place : place + lats]
            spectra = jnp.where(keep, spectra, 0.0)
            fields_of.append(jnp.pad(spectra, ((0, 0), (0, 128 - lats))))
        for r in range(2):
            others = jnp.zeros((bands, 128), F32)
            for p in range(2):
                start = (r * 2 + p) * bands
                one, two = (spectra[start : start + bands] for spectra in fields_of)
                rows[pl.ds((p * 2 + r) * vectors + v, bands, stride=depth), :] = jnp.where(
                    wide < 64, one, pltpu.roll(two, 64, 1)
                )
                for f, spectra in enumerate((one, two)):
                    place = 16 * (p * fields + f)
                    mine = (wide >= place) & (wide < place + 16)
                    others = jnp.where(mine, pltpu.roll(spectra, (place + 64) % 128, 1), others)
            rows[pl.ds((4 + r) * vectors + v, bands, stride=depth), :] = others
    out_ref[...] = rows[...].astype(BF16).reshape(out_ref.shape)


def legendre_kernel(own_ref, rows_ref, even_t_ref, odd_ref, send_ref, even_ref, odd_out_ref, fold):
    bands = rows_ref.shape[0]
    half_bands = bands // 2
    hemisphere = odd_ref.shape[1]
    lats = hemisphere // half_bands
    total_lat = 2 * hemisphere
    depth = fold.shape[1]
    own = own_ref[0:1, 0:1]

    def slab(band):
        packed = rows_ref[FOURIER_BANDS.index(band)].astype(F32)
        others = packed[2 * depth // 4 :]
        groups = []
        for p in range(2):
            for f in range(2):
                main = packed[p * depth // 4 : (p + 1) * depth // 4]
                main = pltpu.roll(main, 64, 1) if f else main
                groups.append(jnp.where(low, main, pltpu.roll(others, 64 - 16 * (p * 2 + f), 1)))
        return jnp.concatenate(groups, axis=0)

    ri = lax.broadcasted_iota(jnp.int32, (128, 128), 0)
    ci = lax.broadcasted_iota(jnp.int32, (128, 128), 1)
    low = ci[: depth // 4] < 64
    mirror = jnp.where(ri + ci == lats - 1, 1.0, 0.0).astype(BF16)
    south = jnp.concatenate([slab(b) for b in range(half_bands, bands)], axis=0).astype(BF16)
    south = lax.dot_general(south, mirror, NN, preferred_element_type=F32)
    for b in range(half_bands):
        north_b = slab(b)
        s = half_bands - 1 - b
        south_b = south[s * depth : (s + 1) * depth]
        fold[0, :, lats * b : lats * (b + 1)] = (north_b + south_b)[:, :lats]
        fold[1, :, lats * b : lats * (b + 1)] = (north_b - south_b)[:, :lats]
    sym, anti = fold[0].astype(BF16), fold[1].astype(BF16)
    even_all = lax.dot_general(sym, even_t_ref[0], NT, preferred_element_type=F32)
    odd_all = lax.dot_general(anti, odd_ref[0], NN, preferred_element_type=F32)
    half = depth // 2
    even_col = lax.broadcasted_iota(jnp.int32, (half, hemisphere + 1), 1)
    odd_col = lax.broadcasted_iota(jnp.int32, (half, hemisphere), 1)
    even = jnp.where(even_col < ((total_lat + 1 - own) >> 1), even_all[:half], even_all[half:])
    odd = jnp.where(odd_col < ((total_lat - own) >> 1), odd_all[:half], odd_all[half:])
    even_ref[...] = even
    odd_out_ref[...] = odd
    tiles = hemisphere // 128
    vectors = 4
    parts = half // vectors
    columns = 2 * send_ref.shape[0] // parts
    last = jnp.broadcast_to(even[:, hemisphere : hemisphere + 1], (half, 128))
    last = jnp.where(lax.broadcasted_iota(jnp.int32, (half, 128), 1) == 0, last, 0.0)
    pieces = [even[:, 128 * i : 128 * (i + 1)] for i in range(tiles)] + [last]
    pieces += [odd[:, 128 * i : 128 * (i + 1)] for i in range(tiles)] + [jnp.zeros_like(last)]
    first = lax.broadcasted_iota(jnp.int32, (8, 128), 0) < vectors
    for fr in range(parts):
        base = fr // 2 * 8
        same = [piece[base : base + 8] for piece in pieces]
        other = [pltpu.roll(piece, vectors, 0) for piece in same]
        low, high = (same, other) if fr % 2 == 0 else (other, same)
        eights = [jnp.where(first, low[i], high[i + 1]) for i in range(0, len(pieces), 2)]
        block = jnp.concatenate(eights, axis=0).astype(BF16)
        for place, (x, _) in enumerate(TILE_PAIRS):
            if x == fr:
                send_ref[place] = block


def gram_kernel(columns, tiles_ref, out_ref, gram_ref):
    pairs, depth, _ = tiles_ref.shape
    wide = pairs // (columns // 2)
    places = [TILE_PAIRS.index((x, z)) for x in range(wide) for z in range(columns // 2)]
    slabs = jnp.stack([tiles_ref[n] for n in places]).astype(F32)
    eights = [slabs[:, 8 * k : 8 * (k + 1)] for k in range(depth // 8)]
    half = len(eights) // 2
    first = lax.broadcasted_iota(jnp.int32, (pairs, 8, 128), 1) < 4
    quarters = []
    for one, two in zip(eights[:half], eights[half:]):
        quarters.append(jnp.where(first, one, pltpu.roll(two, 4, 1)))
        quarters.append(jnp.where(first, pltpu.roll(one, 4, 1), two))
    both = [quarter.reshape(8 * pairs, 128).astype(BF16) for quarter in quarters]
    both = jnp.concatenate(both, axis=1)
    gram = lax.dot_general(both, both, NT, preferred_element_type=F32)
    gram_ref[...] = gram.reshape(gram_ref.shape)
    own = lax.div(lax.axis_index("z"), 2)
    blocks = [gram_ref[x, own].astype(BF16) for x in PRODUCT_XS]
    for n in range(out_ref.shape[0]):
        out_ref[n] = blocks[n % wide]


def finish_kernel(scale, parts_ref, even_in_ref, odd_in_ref, inner_ref, even_ref, odd_ref):
    _, vectors, fields, parts, _ = even_ref.shape
    for f in range(fields):
        for r in range(parts):
            for v in range(vectors):
                row = (f * parts + r) * vectors + v
                even_ref[0, v, f, r : r + 1, :] = even_in_ref[row : row + 1]
                odd_ref[0, v, f, r : r + 1, :] = odd_in_ref[row : row + 1]
    total = jnp.sum(parts_ref[...].astype(F32), axis=0)
    inner_ref[...] = (total[:vectors] + total[vectors:]) * scale


VMEM = pl.BlockSpec(memory_space=pltpu.VMEM)
HBM = pl.BlockSpec(memory_space=pltpu.HBM)
PARAMS = pltpu.CompilerParams(vmem_limit_bytes=32 * 1024 * 1024)


def in_hbm(array):
    return pltpu.with_memory_space_constraint(array, pltpu.HBM)


def fourier(wlist, trunc, grid):
    vectors, fields, lats, lons = grid.shape
    bands = wlist.shape[0]
    depth = 6 * vectors
    table, keep, own = pl.pallas_call(
        functools.partial(table_kernel, lats, lons),
        name="table",
        out_shape=(
            jax.ShapeDtypeStruct((4 * bands, lons), BF16),
            jax.ShapeDtypeStruct((4 * bands, lats), F32),
            jax.ShapeDtypeStruct((8, 128), jnp.int32),
        ),
        in_specs=[HBM, HBM],
        out_specs=(VMEM, VMEM, VMEM),
        scratch_shapes=[
            pltpu.SMEM((bands,), jnp.int32),
            pltpu.VMEM((1, lats), jnp.int32),
            pltpu.SemaphoreType.DMA((2,)),
        ],
        compiler_params=PARAMS,
    )(in_hbm(wlist), in_hbm(trunc.reshape(1, lats)))
    spectra = lax.dot_general(table, grid.reshape(-1, lons), NT, preferred_element_type=F32)
    lat_rows = pl.pallas_call(
        pack_kernel,
        name="pack",
        out_shape=jax.ShapeDtypeStruct((bands, depth, 128), BF16),
        in_specs=[VMEM, VMEM],
        out_specs=VMEM,
        scratch_shapes=[pltpu.VMEM((bands * depth, 128), F32)],
        compiler_params=PARAMS,
    )(spectra, keep)
    return lat_rows, own


def legendre(own, received, leg_even, leg_odd, vectors, tans):
    depth = 8 * vectors
    hemisphere = leg_odd.shape[2]
    return pl.pallas_call(
        legendre_kernel,
        name="legendre",
        out_shape=(
            jax.ShapeDtypeStruct((tans // 2, 2 * (hemisphere // 128 + 1) * vectors, 128), BF16),
            jax.ShapeDtypeStruct((depth // 2, leg_even.shape[2]), F32),
            jax.ShapeDtypeStruct((depth // 2, leg_odd.shape[2]), F32),
        ),
        in_specs=[VMEM] * 4,
        out_specs=(VMEM, VMEM, VMEM),
        scratch_shapes=[pltpu.VMEM((2, depth, hemisphere), F32)],
        compiler_params=PARAMS,
    )(own, received, jnp.swapaxes(leg_even, 1, 2), leg_odd)


def gram(tiles, columns, bands, vectors):
    tans = 2 * tiles.shape[0]
    wide = tans // columns
    return pl.pallas_call(
        functools.partial(gram_kernel, columns),
        name="gram",
        out_shape=jax.ShapeDtypeStruct((bands * wide, 2 * vectors, vectors * tans), BF16),
        in_specs=[VMEM],
        out_specs=VMEM,
        scratch_shapes=[pltpu.VMEM((wide, columns // 2, 2 * vectors, vectors * tans), F32)],
        compiler_params=PARAMS,
    )(tiles)


def finish(products, even, odd, scale, vectors, fields):
    return pl.pallas_call(
        functools.partial(finish_kernel, scale),
        name="finish",
        out_shape=(
            jax.ShapeDtypeStruct((vectors, products.shape[2]), F32),
            jax.ShapeDtypeStruct((1, vectors, fields, 2, even.shape[1]), F32),
            jax.ShapeDtypeStruct((1, vectors, fields, 2, odd.shape[1]), F32),
        ),
        in_specs=[VMEM] * 3,
        out_specs=(VMEM, VMEM, VMEM),
        compiler_params=PARAMS,
    )(products, even, odd)


def on_device(grid, trunc, wlist, leg_even, leg_odd):
    bands = lax.axis_size("band")
    columns = lax.axis_size("z")
    tans = lax.axis_size(("x", "z"))
    vectors, fields, lats, _ = grid.shape
    total_lat = lats * bands
    lat_rows, own = fourier(wlist, trunc, grid)
    received = lax.all_to_all(
        lat_rows, "band", 0, 0, axis_index_groups=[FOURIER_BANDS], tiled=True
    )
    tiles, even, odd = legendre(own, received, leg_even, leg_odd, vectors, tans)
    slab = tiles.shape
    tiles = tiles.reshape(tans, slab[1] // 4, 2, 128)
    wide = tans // columns
    tan_group = [x * columns + 2 * z + n for x, z in TILE_PAIRS for n in range(2)]
    tiles = lax.all_to_all(tiles, ("x", "z"), 0, 0, axis_index_groups=[tan_group], tiled=True)
    products = gram(tiles.reshape(slab), columns, bands, vectors)
    products = products.reshape(-1, vectors, vectors * tans)
    product_groups = [
        [(b * wide + x) * columns + z + n for b in PRODUCT_BANDS for x in PRODUCT_XS for n in range(2)]
        for z in range(0, columns, 2)
    ]
    products = lax.all_to_all(products, ("band", "x", "z"), 0, 0, axis_index_groups=product_groups, tiled=True)
    products = products.reshape(-1, 2 * vectors, vectors * tans)
    scale = 1.0 / (bands * 4.0 * (total_lat + 1))
    inner, even, odd = finish(products, even, odd, scale, vectors, fields)
    return (even, odd, inner.T)


def solution(mesh):
    bands, tans = mesh.devices.shape
    split = jax.sharding.Mesh(mesh.devices.reshape(bands, 4, tans // 4), ("band", "x", "z"))
    tan = ("x", "z")
    return jax.shard_map(
        on_device,
        mesh=split,
        in_specs=(
            P(tan, None, "band", None),
            P("band"),
            P(),
            P("band", None, None),
            P("band", None, None),
        ),
        out_specs=(
            P("band", tan, None, None, None),
            P("band", tan, None, None, None),
            P(None, tan),
        ),
        check_vma=False,
    )
```

```python
import functools
import math

import jax
import jax.numpy as jnp
from jax import lax
from jax.experimental import pallas as pl
from jax.experimental.pallas import tpu as pltpu
from jax.sharding import PartitionSpec as P

F32 = jnp.float32
FOURIER_BANDS = [11, 12, 13, 14, 15, 0, 1, 2, 3, 4, 5, 6, 7, 8, 9, 10]
TILE_PAIRS = [
    (2, 3), (1, 3), (3, 3), (0, 3), (2, 0), (2, 2), (1, 0), (1, 2),
    (3, 0), (3, 2), (0, 0), (0, 2), (2, 1), (1, 1), (3, 1), (0, 1),
]
PRODUCT_BANDS = [11, 2, 3, 0, 4, 1, 5, 6, 14, 7, 15, 8, 12, 9, 13, 10]
PRODUCT_XS = [2, 0, 1, 3]
BF16 = jnp.bfloat16
NT = (((1,), (1,)), ((), ()))
NN = (((1,), (0,)), ((), ()))


def cos_sin(phase, count):
    phase = phase % count
    quarter = count // 4
    turn = (phase + quarter // 2) // quarter
    angle = (phase - turn * quarter).astype(F32) * (2.0 * math.pi / count)
    square = angle * angle
    cos = 1.0 + square * (-1 / 2 + square * (1 / 24 + square * (-1 / 720 + square * (1 / 40320))))
    sin = angle * (1.0 + square * (-1 / 6 + square * (1 / 120 + square * (-1 / 5040 + square * (1 / 362880)))))
    odd = (turn & 1) == 1
    cos, sin = jnp.where(odd, sin, cos), jnp.where(odd, cos, sin)
    return jnp.where(((turn + 1) & 2) == 2, -cos, cos), jnp.where((turn & 2) == 2, -sin, sin)


def fourier_kernel(wlist_hbm, trunc_hbm, grid_hbm, out_ref, own_ref, wlist_ref, trunc_ref, grid_ref, table, rows, small, sems):
    vectors, fields, lats, lons = grid_ref.shape
    bands = wlist_ref.shape[0]
    total_lat = lats * bands
    members = 2 * bands
    get_wlist = pltpu.make_async_copy(wlist_hbm, wlist_ref, small.at[0])
    get_trunc = pltpu.make_async_copy(trunc_hbm, trunc_ref, small.at[1])
    get_wlist.start()
    get_trunc.start()
    half = vectors // 2
    fetches = [
        pltpu.make_async_copy(grid_hbm.at[pl.ds(v, half)], grid_ref.at[pl.ds(v, half)], sems.at[n])
        for n, v in enumerate(range(0, vectors, half))
    ]
    for fetch in fetches:
        fetch.start()
    row = lax.broadcasted_iota(jnp.int32, (members, 128), 0)
    lane = lax.broadcasted_iota(jnp.int32, (members, 128), 1)
    get_wlist.wait()
    mvals = jnp.zeros((members, 128), jnp.int32)
    for b in range(bands):
        wave, place = wlist_ref[b], FOURIER_BANDS.index(b)
        mvals = jnp.where(row == place, wave, mvals)
        mvals = jnp.where(row == bands + place, total_lat - 1 - wave, mvals)
    own_ref[...] = jnp.full(own_ref.shape, wlist_ref[lax.axis_index("band")], jnp.int32)
    scaling = 1.0 / math.sqrt(lons)
    chunks = lons // 128
    fine_cos, fine_sin = cos_sin(mvals * lane, lons)
    coarse_cos, coarse_sin = cos_sin(mvals * lane, chunks)
    coarse_cos, coarse_sin = coarse_cos * scaling, coarse_sin * scaling
    for i in range(chunks):
        cc, cs = coarse_cos[:, i : i + 1], coarse_sin[:, i : i + 1]
        table[:members, 128 * i : 128 * (i + 1)] = (cc * fine_cos - cs * fine_sin).astype(BF16)
        table[members:, 128 * i : 128 * (i + 1)] = (-(cs * fine_cos + cc * fine_sin)).astype(BF16)
    get_trunc.wait()
    keep = mvals[:, :lats] <= trunc_ref[...]
    keep = jnp.concatenate([keep, keep], axis=0)
    depth = out_ref.shape[1]
    wide = lax.broadcasted_iota(jnp.int32, (bands, 128), 1)
    for v in range(vectors):
        if v % half == 0:
            fetches[v // half].wait()
        fields_of = []
        for f in range(fields):
            spectra = lax.dot_general(table[...], grid_ref[v, f], NT, preferred_element_type=F32)
            spectra = jnp.where(keep, spectra, 0.0)
            fields_of.append(jnp.pad(spectra, ((0, 0), (0, 128 - lats))))
        for r in range(2):
            others = jnp.zeros((bands, 128), F32)
            for p in range(2):
                start = (r * 2 + p) * bands
                one, two = (spectra[start : start + bands] for spectra in fields_of)
                rows[pl.ds((p * 2 + r) * vectors + v, bands, stride=depth), :] = jnp.where(
                    wide < 64, one, pltpu.roll(two, 64, 1)
                )
                for f, spectra in enumerate((one, two)):
                    place = 16 * (p * fields + f)
                    mine = (wide >= place) & (wide < place + 16)
                    others = jnp.where(mine, pltpu.roll(spectra, (place + 64) % 128, 1), others)
            rows[pl.ds((4 + r) * vectors + v, bands, stride=depth), :] = others
    out_ref[...] = rows[...].astype(BF16).reshape(out_ref.shape)


def legendre_kernel(own_ref, rows_ref, even_t_ref, odd_ref, send_ref, even_ref, odd_out_ref, fold):
    bands = rows_ref.shape[0]
    half_bands = bands // 2
    hemisphere = odd_ref.shape[1]
    lats = hemisphere // half_bands
    total_lat = 2 * hemisphere
    depth = fold.shape[1]
    own = own_ref[0:1, 0:1]

    def slab(band):
        packed = rows_ref[FOURIER_BANDS.index(band)].astype(F32)
        others = packed[2 * depth // 4 :]
        groups = []
        for p in range(2):
            for f in range(2):
                main = packed[p * depth // 4 : (p + 1) * depth // 4]
                main = pltpu.roll(main, 64, 1) if f else main
                groups.append(jnp.where(low, main, pltpu.roll(others, 64 - 16 * (p * 2 + f), 1)))
        return jnp.concatenate(groups, axis=0)

    ri = lax.broadcasted_iota(jnp.int32, (128, 128), 0)
    ci = lax.broadcasted_iota(jnp.int32, (128, 128), 1)
    low = ci[: depth // 4] < 64
    mirror = jnp.where(ri + ci == lats - 1, 1.0, 0.0).astype(BF16)
    south = jnp.concatenate([slab(b) for b in range(half_bands, bands)], axis=0).astype(BF16)
    south = lax.dot_general(south, mirror, NN, preferred_element_type=F32)
    for b in range(half_bands):
        north_b = slab(b)
        s = half_bands - 1 - b
        south_b = south[s * depth : (s + 1) * depth]
        fold[0, :, lats * b : lats * (b + 1)] = (north_b + south_b)[:, :lats]
        fold[1, :, lats * b : lats * (b + 1)] = (north_b - south_b)[:, :lats]
    sym, anti = fold[0].astype(BF16), fold[1].astype(BF16)
    even_all = lax.dot_general(sym, even_t_ref[0], NT, preferred_element_type=F32)
    odd_all = lax.dot_general(anti, odd_ref[0], NN, preferred_element_type=F32)
    half = depth // 2
    even_col = lax.broadcasted_iota(jnp.int32, (half, hemisphere + 1), 1)
    odd_col = lax.broadcasted_iota(jnp.int32, (half, hemisphere), 1)
    even = jnp.where(even_col < ((total_lat + 1 - own) >> 1), even_all[:half], even_all[half:])
    odd = jnp.where(odd_col < ((total_lat - own) >> 1), odd_all[:half], odd_all[half:])
    even_ref[...] = even
    odd_out_ref[...] = odd
    tiles = hemisphere // 128
    vectors = 4
    parts = half // vectors
    columns = 2 * send_ref.shape[0] // parts
    last = jnp.broadcast_to(even[:, hemisphere : hemisphere + 1], (half, 128))
    last = jnp.where(lax.broadcasted_iota(jnp.int32, (half, 128), 1) == 0, last, 0.0)
    pieces = [even[:, 128 * i : 128 * (i + 1)] for i in range(tiles)] + [last]
    pieces += [odd[:, 128 * i : 128 * (i + 1)] for i in range(tiles)] + [jnp.zeros_like(last)]
    first = lax.broadcasted_iota(jnp.int32, (8, 128), 0) < vectors
    for fr in range(parts):
        base = fr // 2 * 8
        same = [piece[base : base + 8] for piece in pieces]
        other = [pltpu.roll(piece, vectors, 0) for piece in same]
        low, high = (same, other) if fr % 2 == 0 else (other, same)
        eights = [jnp.where(first, low[i], high[i + 1]) for i in range(0, len(pieces), 2)]
        block = jnp.concatenate(eights, axis=0).astype(BF16)
        for place, (x, _) in enumerate(TILE_PAIRS):
            if x == fr:
                send_ref[place] = block


def gram_kernel(columns, tiles_ref, out_ref, gram_ref):
    pairs, depth, _ = tiles_ref.shape
    wide = pairs // (columns // 2)
    places = [TILE_PAIRS.index((x, z)) for x in range(wide) for z in range(columns // 2)]
    slabs = jnp.stack([tiles_ref[n] for n in places]).astype(F32)
    eights = [slabs[:, 8 * k : 8 * (k + 1)] for k in range(depth // 8)]
    half = len(eights) // 2
    first = lax.broadcasted_iota(jnp.int32, (pairs, 8, 128), 1) < 4
    quarters = []
    for one, two in zip(eights[:half], eights[half:]):
        quarters.append(jnp.where(first, one, pltpu.roll(two, 4, 1)))
        quarters.append(jnp.where(first, pltpu.roll(one, 4, 1), two))
    both = [quarter.reshape(8 * pairs, 128).astype(BF16) for quarter in quarters]
    both = jnp.concatenate(both, axis=1)
    gram = lax.dot_general(both, both, NT, preferred_element_type=F32)
    gram_ref[...] = gram.reshape(gram_ref.shape)
    own = lax.div(lax.axis_index("z"), 2)
    blocks = [gram_ref[x, own].astype(BF16) for x in PRODUCT_XS]
    for n in range(out_ref.shape[0]):
        out_ref[n] = blocks[n % wide]


def finish_kernel(scale, parts_ref, even_in_ref, odd_in_ref, inner_ref, even_ref, odd_ref):
    _, vectors, fields, parts, _ = even_ref.shape
    for f in range(fields):
        for r in range(parts):
            for v in range(vectors):
                row = (f * parts + r) * vectors + v
                even_ref[0, v, f, r : r + 1, :] = even_in_ref[row : row + 1]
                odd_ref[0, v, f, r : r + 1, :] = odd_in_ref[row : row + 1]
    total = jnp.sum(parts_ref[...].astype(F32), axis=0)
    inner_ref[...] = (total[:vectors] + total[vectors:]) * scale


VMEM = pl.BlockSpec(memory_space=pltpu.VMEM)
HBM = pl.BlockSpec(memory_space=pltpu.HBM)
PARAMS = pltpu.CompilerParams(vmem_limit_bytes=32 * 1024 * 1024)


def in_hbm(array):
    return pltpu.with_memory_space_constraint(array, pltpu.HBM)


def fourier(wlist, trunc, grid):
    vectors, fields, lats, lons = grid.shape
    bands = wlist.shape[0]
    depth = 6 * vectors
    return pl.pallas_call(
        fourier_kernel,
        name="fourier",
        out_shape=(
            jax.ShapeDtypeStruct((bands, depth, 128), BF16),
            jax.ShapeDtypeStruct((8, 128), jnp.int32),
        ),
        in_specs=[HBM, HBM, HBM],
        out_specs=(VMEM, VMEM),
        scratch_shapes=[
            pltpu.SMEM((bands,), jnp.int32),
            pltpu.VMEM((1, lats), jnp.int32),
            pltpu.VMEM(grid.shape, BF16),
            pltpu.VMEM((4 * bands, lons), BF16),
            pltpu.VMEM((bands * depth, 128), F32),
            pltpu.SemaphoreType.DMA((2,)),
            pltpu.SemaphoreType.DMA((2,)),
        ],
        compiler_params=PARAMS,
    )(in_hbm(wlist), in_hbm(trunc.reshape(1, lats)), in_hbm(grid))


def legendre(own, received, leg_even, leg_odd, vectors, tans):
    depth = 8 * vectors
    hemisphere = leg_odd.shape[2]
    return pl.pallas_call(
        legendre_kernel,
        name="legendre",
        out_shape=(
            jax.ShapeDtypeStruct((tans // 2, 2 * (hemisphere // 128 + 1) * vectors, 128), BF16),
            jax.ShapeDtypeStruct((depth // 2, leg_even.shape[2]), F32),
            jax.ShapeDtypeStruct((depth // 2, leg_odd.shape[2]), F32),
        ),
        in_specs=[VMEM] * 4,
        out_specs=(VMEM, VMEM, VMEM),
        scratch_shapes=[pltpu.VMEM((2, depth, hemisphere), F32)],
        compiler_params=PARAMS,
    )(own, received, jnp.swapaxes(leg_even, 1, 2), leg_odd)


def gram(tiles, columns, bands, vectors):
    tans = 2 * tiles.shape[0]
    wide = tans // columns
    return pl.pallas_call(
        functools.partial(gram_kernel, columns),
        name="gram",
        out_shape=jax.ShapeDtypeStruct((bands * wide, 2 * vectors, vectors * tans), BF16),
        in_specs=[VMEM],
        out_specs=VMEM,
        scratch_shapes=[pltpu.VMEM((wide, columns // 2, 2 * vectors, vectors * tans), F32)],
        compiler_params=PARAMS,
    )(tiles)


def finish(products, even, odd, scale, vectors, fields):
    return pl.pallas_call(
        functools.partial(finish_kernel, scale),
        name="finish",
        out_shape=(
            jax.ShapeDtypeStruct((vectors, products.shape[2]), F32),
            jax.ShapeDtypeStruct((1, vectors, fields, 2, even.shape[1]), F32),
            jax.ShapeDtypeStruct((1, vectors, fields, 2, odd.shape[1]), F32),
        ),
        in_specs=[VMEM] * 3,
        out_specs=(VMEM, VMEM, VMEM),
        compiler_params=PARAMS,
    )(products, even, odd)


def on_device(grid, trunc, wlist, leg_even, leg_odd):
    bands = lax.axis_size("band")
    columns = lax.axis_size("z")
    tans = lax.axis_size(("x", "z"))
    vectors, fields, lats, _ = grid.shape
    total_lat = lats * bands
    lat_rows, own = fourier(wlist, trunc, grid)
    received = lax.all_to_all(
        lat_rows, "band", 0, 0, axis_index_groups=[FOURIER_BANDS], tiled=True
    )
    tiles, even, odd = legendre(own, received, leg_even, leg_odd, vectors, tans)
    slab = tiles.shape
    tiles = tiles.reshape(tans, slab[1] // 4, 2, 128)
    wide = tans // columns
    tan_group = [x * columns + 2 * z + n for x, z in TILE_PAIRS for n in range(2)]
    tiles = lax.all_to_all(tiles, ("x", "z"), 0, 0, axis_index_groups=[tan_group], tiled=True)
    products = gram(tiles.reshape(slab), columns, bands, vectors)
    products = products.reshape(-1, vectors, vectors * tans)
    product_groups = [
        [(b * wide + x) * columns + z + n for b in PRODUCT_BANDS for x in PRODUCT_XS for n in range(2)]
        for z in range(0, columns, 2)
    ]
    products = lax.all_to_all(products, ("band", "x", "z"), 0, 0, axis_index_groups=product_groups, tiled=True)
    products = products.reshape(-1, 2 * vectors, vectors * tans)
    scale = 1.0 / (bands * 4.0 * (total_lat + 1))
    inner, even, odd = finish(products, even, odd, scale, vectors, fields)
    return (even, odd, inner.T)


def solution(mesh):
    bands, tans = mesh.devices.shape
    split = jax.sharding.Mesh(mesh.devices.reshape(bands, 4, tans // 4), ("band", "x", "z"))
    tan = ("x", "z")
    return jax.shard_map(
        on_device,
        mesh=split,
        in_specs=(
            P(tan, None, "band", None),
            P("band"),
            P(),
            P("band", None, None),
            P("band", None, None),
        ),
        out_specs=(
            P("band", tan, None, None, None),
            P("band", tan, None, None, None),
            P(None, tan),
        ),
        check_vma=False,
    )
```

```python
import functools
import math

import jax
import jax.numpy as jnp
from jax import lax
from jax.experimental import pallas as pl
from jax.experimental.pallas import tpu as pltpu
from jax.sharding import PartitionSpec as P

F32 = jnp.float32
FOURIER_BANDS = [11, 12, 13, 14, 15, 0, 1, 2, 3, 4, 5, 6, 7, 8, 9, 10]
TILE_PAIRS = [
    (2, 3), (1, 3), (3, 3), (0, 3), (2, 0), (2, 2), (1, 0), (1, 2),
    (3, 0), (3, 2), (0, 0), (0, 2), (2, 1), (1, 1), (3, 1), (0, 1),
]
PRODUCT_BANDS = [11, 2, 3, 0, 4, 1, 5, 6, 14, 7, 15, 8, 12, 9, 13, 10]
PRODUCT_XS = [2, 0, 1, 3]
BF16 = jnp.bfloat16
NT = (((1,), (1,)), ((), ()))
NN = (((1,), (0,)), ((), ()))


def cos_sin(phase, count):
    phase = phase % count
    quarter = count // 4
    turn = (phase + quarter // 2) // quarter
    angle = (phase - turn * quarter).astype(F32) * (2.0 * math.pi / count)
    square = angle * angle
    cos = 1.0 + square * (-1 / 2 + square * (1 / 24 + square * (-1 / 720 + square * (1 / 40320))))
    sin = angle * (1.0 + square * (-1 / 6 + square * (1 / 120 + square * (-1 / 5040 + square * (1 / 362880)))))
    odd = (turn & 1) == 1
    cos, sin = jnp.where(odd, sin, cos), jnp.where(odd, cos, sin)
    return jnp.where(((turn + 1) & 2) == 2, -cos, cos), jnp.where((turn & 2) == 2, -sin, sin)


def fourier_kernel(wlist_hbm, trunc_hbm, grid_hbm, out_ref, own_ref, wlist_ref, trunc_ref, grid_ref, table, rows, small, sems):
    vectors, fields, lats, lons = grid_ref.shape
    bands = wlist_ref.shape[0]
    total_lat = lats * bands
    members = 2 * bands
    get_wlist = pltpu.make_async_copy(wlist_hbm, wlist_ref, small.at[0])
    get_trunc = pltpu.make_async_copy(trunc_hbm, trunc_ref, small.at[1])
    get_wlist.start()
    get_trunc.start()
    half = vectors // 2
    fetches = [
        pltpu.make_async_copy(grid_hbm.at[pl.ds(v, half)], grid_ref.at[pl.ds(v, half)], sems.at[n])
        for n, v in enumerate(range(0, vectors, half))
    ]
    for fetch in fetches:
        fetch.start()
    row = lax.broadcasted_iota(jnp.int32, (members, 128), 0)
    lane = lax.broadcasted_iota(jnp.int32, (members, 128), 1)
    get_wlist.wait()
    mvals = jnp.zeros((members, 128), jnp.int32)
    for b in range(bands):
        wave, place = wlist_ref[b], FOURIER_BANDS.index(b)
        mvals = jnp.where(row == place, wave, mvals)
        mvals = jnp.where(row == bands + place, total_lat - 1 - wave, mvals)
    own_ref[...] = jnp.full(own_ref.shape, wlist_ref[lax.axis_index("band")], jnp.int32)
    scaling = 1.0 / math.sqrt(lons)
    chunks = lons // 128
    fine_cos, fine_sin = cos_sin(mvals * lane, lons)
    coarse_cos, coarse_sin = cos_sin(mvals * lane, chunks)
    coarse_cos, coarse_sin = coarse_cos * scaling, coarse_sin * scaling
    for i in range(chunks):
        cc, cs = coarse_cos[:, i : i + 1], coarse_sin[:, i : i + 1]
        table[:members, 128 * i : 128 * (i + 1)] = (cc * fine_cos - cs * fine_sin).astype(BF16)
        table[members:, 128 * i : 128 * (i + 1)] = (-(cs * fine_cos + cc * fine_sin)).astype(BF16)
    get_trunc.wait()
    keep = mvals[:, :lats] <= trunc_ref[...]
    keep = jnp.concatenate([keep, keep], axis=0)
    depth = out_ref.shape[1] // 2
    wide = lax.broadcasted_iota(jnp.int32, (bands, 128), 1)
    for v in range(vectors):
        if v % half == 0:
            fetches[v // half].wait()
        fields_of = []
        for f in range(fields):
            spectra = lax.dot_general(table[...], grid_ref[v, f], NT, preferred_element_type=F32)
            spectra = jnp.where(keep, spectra, 0.0)
            fields_of.append(jnp.pad(spectra, ((0, 0), (0, 128 - lats))))
        others = jnp.zeros((bands, 128), F32)
        for r in range(2):
            for p in range(2):
                start = (r * 2 + p) * bands
                one, two = (spectra[start : start + bands] for spectra in fields_of)
                rows[pl.ds((p * 2 + r) * vectors + v, bands, stride=depth), :] = jnp.where(
                    wide < 64, one, pltpu.roll(two, 64, 1)
                )
                for f, spectra in enumerate((one, two)):
                    place = 64 * r + 16 * (p * fields + f)
                    mine = (wide >= place) & (wide < place + 16)
                    others = jnp.where(mine, pltpu.roll(spectra, (place + 64) % 128, 1), others)
        rows[pl.ds(4 * vectors + v, bands, stride=depth), :] = others
    out_ref[...] = rows[...].reshape(out_ref.shape).astype(BF16)


def legendre_kernel(own_ref, rows_ref, even_t_ref, odd_ref, send_ref, even_ref, odd_out_ref, fold):
    bands = 2 * rows_ref.shape[0]
    half_bands = bands // 2
    hemisphere = odd_ref.shape[1]
    lats = hemisphere // half_bands
    total_lat = 2 * hemisphere
    depth = fold.shape[1]
    own = own_ref[0:1, 0:1]

    def slab(band):
        place = FOURIER_BANDS.index(band)
        start = place % 2 * (5 * depth // 8)
        packed = rows_ref[place // 2].astype(F32)[start : start + 5 * depth // 8]
        others = packed[depth // 2 :]
        others = jnp.concatenate([others, pltpu.roll(others, 64, 1)], axis=0)
        groups = []
        for p in range(2):
            for f in range(2):
                main = packed[p * depth // 4 : (p + 1) * depth // 4]
                main = pltpu.roll(main, 64, 1) if f else main
                groups.append(jnp.where(low, main, pltpu.roll(others, 64 - 16 * (p * 2 + f), 1)))
        return jnp.concatenate(groups, axis=0)

    ri = lax.broadcasted_iota(jnp.int32, (128, 128), 0)
    ci = lax.broadcasted_iota(jnp.int32, (128, 128), 1)
    low = ci[: depth // 4] < 64
    mirror = jnp.where(ri + ci == lats - 1, 1.0, 0.0).astype(BF16)
    south = jnp.concatenate([slab(b) for b in range(half_bands, bands)], axis=0).astype(BF16)
    south = lax.dot_general(south, mirror, NN, preferred_element_type=F32)
    for b in range(half_bands):
        north_b = slab(b)
        s = half_bands - 1 - b
        south_b = south[s * depth : (s + 1) * depth]
        fold[0, :, lats * b : lats * (b + 1)] = (north_b + south_b)[:, :lats]
        fold[1, :, lats * b : lats * (b + 1)] = (north_b - south_b)[:, :lats]
    sym, anti = fold[0].astype(BF16), fold[1].astype(BF16)
    even_all = lax.dot_general(sym, even_t_ref[0], NT, preferred_element_type=F32)
    odd_all = lax.dot_general(anti, odd_ref[0], NN, preferred_element_type=F32)
    half = depth // 2
    even_col = lax.broadcasted_iota(jnp.int32, (half, hemisphere + 1), 1)
    odd_col = lax.broadcasted_iota(jnp.int32, (half, hemisphere), 1)
    even = jnp.where(even_col < ((total_lat + 1 - own) >> 1), even_all[:half], even_all[half:])
    odd = jnp.where(odd_col < ((total_lat - own) >> 1), odd_all[:half], odd_all[half:])
    even_ref[...] = even
    odd_out_ref[...] = odd
    tiles = hemisphere // 128
    vectors = 4
    parts = half // vectors
    columns = 2 * send_ref.shape[0] // parts
    last = jnp.broadcast_to(even[:, hemisphere : hemisphere + 1], (half, 128))
    last = jnp.where(lax.broadcasted_iota(jnp.int32, (half, 128), 1) == 0, last, 0.0)
    pieces = [even[:, 128 * i : 128 * (i + 1)] for i in range(tiles)] + [last]
    pieces += [odd[:, 128 * i : 128 * (i + 1)] for i in range(tiles)] + [jnp.zeros_like(last)]
    first = lax.broadcasted_iota(jnp.int32, (8, 128), 0) < vectors
    for fr in range(parts):
        base = fr // 2 * 8
        same = [piece[base : base + 8] for piece in pieces]
        other = [pltpu.roll(piece, vectors, 0) for piece in same]
        low, high = (same, other) if fr % 2 == 0 else (other, same)
        eights = [jnp.where(first, low[i], high[i + 1]) for i in range(0, len(pieces), 2)]
        block = jnp.concatenate(eights, axis=0).astype(BF16)
        for place, (x, _) in enumerate(TILE_PAIRS):
            if x == fr:
                send_ref[place] = block


def gram_kernel(columns, tiles_ref, out_ref, gram_ref):
    pairs, depth, _ = tiles_ref.shape
    wide = pairs // (columns // 2)
    places = [TILE_PAIRS.index((x, z)) for x in range(wide) for z in range(columns // 2)]
    slabs = jnp.stack([tiles_ref[n] for n in places]).astype(F32)
    eights = [slabs[:, 8 * k : 8 * (k + 1)] for k in range(depth // 8)]
    half = len(eights) // 2
    first = lax.broadcasted_iota(jnp.int32, (pairs, 8, 128), 1) < 4
    quarters = []
    for one, two in zip(eights[:half], eights[half:]):
        quarters.append(jnp.where(first, one, pltpu.roll(two, 4, 1)))
        quarters.append(jnp.where(first, pltpu.roll(one, 4, 1), two))
    both = [quarter.reshape(8 * pairs, 128).astype(BF16) for quarter in quarters]
    both = jnp.concatenate(both, axis=1)
    gram = lax.dot_general(both, both, NT, preferred_element_type=F32)
    gram_ref[...] = gram.reshape(gram_ref.shape)
    own = lax.div(lax.axis_index("z"), 2)
    blocks = [gram_ref[x, own].astype(BF16) for x in PRODUCT_XS]
    for n in range(out_ref.shape[0]):
        out_ref[n] = blocks[n % wide]


def finish_kernel(scale, parts_ref, even_in_ref, odd_in_ref, inner_ref, even_ref, odd_ref):
    _, vectors, fields, parts, _ = even_ref.shape
    for f in range(fields):
        for r in range(parts):
            for v in range(vectors):
                row = (f * parts + r) * vectors + v
                even_ref[0, v, f, r : r + 1, :] = even_in_ref[row : row + 1]
                odd_ref[0, v, f, r : r + 1, :] = odd_in_ref[row : row + 1]
    total = jnp.sum(parts_ref[...].astype(F32), axis=0)
    inner_ref[...] = (total[:vectors] + total[vectors:]) * scale


VMEM = pl.BlockSpec(memory_space=pltpu.VMEM)
HBM = pl.BlockSpec(memory_space=pltpu.HBM)
PARAMS = pltpu.CompilerParams(vmem_limit_bytes=32 * 1024 * 1024)


def in_hbm(array):
    return pltpu.with_memory_space_constraint(array, pltpu.HBM)


def fourier(wlist, trunc, grid):
    vectors, fields, lats, lons = grid.shape
    bands = wlist.shape[0]
    depth = 5 * vectors
    return pl.pallas_call(
        fourier_kernel,
        name="fourier",
        out_shape=(
            jax.ShapeDtypeStruct((bands // 2, 2 * depth, 128), BF16),
            jax.ShapeDtypeStruct((8, 128), jnp.int32),
        ),
        in_specs=[HBM, HBM, HBM],
        out_specs=(VMEM, VMEM),
        scratch_shapes=[
            pltpu.SMEM((bands,), jnp.int32),
            pltpu.VMEM((1, lats), jnp.int32),
            pltpu.VMEM(grid.shape, BF16),
            pltpu.VMEM((4 * bands, lons), BF16),
            pltpu.VMEM((bands * depth, 128), F32),
            pltpu.SemaphoreType.DMA((2,)),
            pltpu.SemaphoreType.DMA((2,)),
        ],
        compiler_params=PARAMS,
    )(in_hbm(wlist), in_hbm(trunc.reshape(1, lats)), in_hbm(grid))


def legendre(own, received, leg_even, leg_odd, vectors, tans):
    depth = 8 * vectors
    hemisphere = leg_odd.shape[2]
    return pl.pallas_call(
        legendre_kernel,
        name="legendre",
        out_shape=(
            jax.ShapeDtypeStruct((tans // 2, 2 * (hemisphere // 128 + 1) * vectors, 128), BF16),
            jax.ShapeDtypeStruct((depth // 2, leg_even.shape[2]), F32),
            jax.ShapeDtypeStruct((depth // 2, leg_odd.shape[2]), F32),
        ),
        in_specs=[VMEM] * 4,
        out_specs=(VMEM, VMEM, VMEM),
        scratch_shapes=[pltpu.VMEM((2, depth, hemisphere), F32)],
        compiler_params=PARAMS,
    )(own, received, jnp.swapaxes(leg_even, 1, 2), leg_odd)


def gram(tiles, columns, bands, vectors):
    tans = 2 * tiles.shape[0]
    wide = tans // columns
    return pl.pallas_call(
        functools.partial(gram_kernel, columns),
        name="gram",
        out_shape=jax.ShapeDtypeStruct((bands * wide, 2 * vectors, vectors * tans), BF16),
        in_specs=[VMEM],
        out_specs=VMEM,
        scratch_shapes=[pltpu.VMEM((wide, columns // 2, 2 * vectors, vectors * tans), F32)],
        compiler_params=PARAMS,
    )(tiles)


def finish(products, even, odd, scale, vectors, fields):
    return pl.pallas_call(
        functools.partial(finish_kernel, scale),
        name="finish",
        out_shape=(
            jax.ShapeDtypeStruct((vectors, products.shape[2]), F32),
            jax.ShapeDtypeStruct((1, vectors, fields, 2, even.shape[1]), F32),
            jax.ShapeDtypeStruct((1, vectors, fields, 2, odd.shape[1]), F32),
        ),
        in_specs=[VMEM] * 3,
        out_specs=(VMEM, VMEM, VMEM),
        compiler_params=PARAMS,
    )(products, even, odd)


def on_device(grid, trunc, wlist, leg_even, leg_odd):
    bands = lax.axis_size("band")
    columns = lax.axis_size("z")
    tans = lax.axis_size(("x", "z"))
    vectors, fields, lats, _ = grid.shape
    total_lat = lats * bands
    lat_rows, own = fourier(wlist, trunc, grid)
    slabs = lat_rows.shape
    lat_rows = lat_rows.reshape(bands, 5, vectors, 128)
    received = lax.all_to_all(lat_rows, "band", 0, 0, axis_index_groups=[FOURIER_BANDS], tiled=True)
    received = received.reshape(slabs)
    tiles, even, odd = legendre(own, received, leg_even, leg_odd, vectors, tans)
    slab = tiles.shape
    tiles = tiles.reshape(tans, slab[1] // 4, 2, 128)
    wide = tans // columns
    tan_group = [x * columns + 2 * z + n for x, z in TILE_PAIRS for n in range(2)]
    tiles = lax.all_to_all(tiles, ("x", "z"), 0, 0, axis_index_groups=[tan_group], tiled=True)
    products = gram(tiles.reshape(slab), columns, bands, vectors)
    products = products.reshape(-1, vectors, vectors * tans)
    product_groups = [
        [(b * wide + x) * columns + z + n for b in PRODUCT_BANDS for x in PRODUCT_XS for n in range(2)]
        for z in range(0, columns, 2)
    ]
    products = lax.all_to_all(products, ("band", "x", "z"), 0, 0, axis_index_groups=product_groups, tiled=True)
    products = products.reshape(-1, 2 * vectors, vectors * tans)
    scale = 1.0 / (bands * 4.0 * (total_lat + 1))
    inner, even, odd = finish(products, even, odd, scale, vectors, fields)
    return (even, odd, inner.T)


def solution(mesh):
    bands, tans = mesh.devices.shape
    split = jax.sharding.Mesh(mesh.devices.reshape(bands, 4, tans // 4), ("band", "x", "z"))
    tan = ("x", "z")
    return jax.shard_map(
        on_device,
        mesh=split,
        in_specs=(
            P(tan, None, "band", None),
            P("band"),
            P(),
            P("band", None, None),
            P("band", None, None),
        ),
        out_specs=(
            P("band", tan, None, None, None),
            P("band", tan, None, None, None),
            P(None, tan),
        ),
        check_vma=False,
    )
```
